32 devices in a mesh: pipe: 2 (over core), dp: 16 (over z, y, x).
Axes of the slice: x: 2, y: 2, z: 4, core: 2. Of those that a mesh axis runs over, the one named last changes fastest.
Arguments:
- entities: bfloat16 [512, 512, 256], P(('pipe', 'dp')), may hold values from -6 to 6
- counts: int32 [512], P(('pipe', 'dp')), may hold values from 20 to 512, as said below
- order: int32 [512], P(('pipe', 'dp')), may hold values from 0 to 511, as said below
- first_gain: float32 [256], replicated, may hold values from 0.5 to 1.5
- first_shift: float32 [256], replicated, may hold values from -1.75 to 1.75
- attend_in: bfloat16 [256, 768], replicated, may hold values from -0.375 to 0.375
- attend_out: bfloat16 [256, 256], replicated, may hold values from -3 to 3
- second_gain: float32 [256], replicated, may hold values from 0.5 to 1.5
- second_shift: float32 [256], replicated, may hold values from -1.75 to 1.75
- up_weight: bfloat16 [256, 1024], replicated, may hold values from -0.375 to 0.375
- up_bias: float32 [1024], replicated, may hold values from -3 to 3
- down_weight: bfloat16 [1024, 256], replicated, may hold values from -0.1875 to 0.1875
- down_bias: float32 [256], replicated, may hold values from -1.75 to 1.75
- core_input: bfloat16 [256, 1536], replicated, may hold values from -1.5 to 1.5
- core_upper: bfloat16 [2, 384, 1536], replicated, may hold values from -0.625 to 0.625
- core_loop: bfloat16 [3, 384, 1536], replicated, may hold values from -0.3125 to 0.3125
- core_first_bias: float32 [1536], replicated, may hold values from -3 to 3
- core_upper_bias: float32 [2, 1536], replicated, may hold values from -3 to 3
- core_grad: bfloat16 [512, 384], P(('pipe', 'dp')), may hold values from -6 to 6
Outputs:
- core_out: bfloat16 [512, 384], P(('pipe', 'dp'))
- entity_grad: bfloat16 [512, 512, 256], P(('pipe', 'dp'))
- first_gain_gradient: float32 [256], replicated
- first_shift_gradient: float32 [256], replicated
- attend_in_gradient: float32 [256, 768], replicated
- attend_out_gradient: float32 [256, 256], replicated
- second_gain_gradient: float32 [256], replicated
- second_shift_gradient: float32 [256], replicated
- up_weight_gradient: float32 [256, 1024], replicated
- up_bias_gradient: float32 [1024], replicated
- down_weight_gradient: float32 [1024, 256], replicated
- down_bias_gradient: float32 [256], replicated
- core_input_gradient: float32 [256, 1536], replicated
- core_upper_gradient: float32 [2, 384, 1536], replicated
- core_loop_gradient: float32 [3, 384, 1536], replicated
- core_first_bias_gradient: float32 [1536], replicated
- core_upper_bias_gradient: float32 [2, 1536], replicated
The draws below stay inside these ranges and needn't reach their ends.
Inputs may be any that keep to these rules, and one draw needn't show every extreme that they name: entities present in a frame; slots from counts onward are padding. The game in rows [r, r + 8) of order, r a multiple of 8, holds the frames [s, s + 8) in some order, where s = (r + 256) modulo 512.
All inputs are finite; a program needn't handle non-finite values.
Results may differ from the reference program's by a relative error of at most 0.03.
The reference program's roundings to bfloat16 on the way count: a program that leaves them out, or rounds other values in their place, can miss the bound.
Values may be sent and summed in bfloat16 or wider, within the bound.
A program may use at most 320 MiB of HBM per device.

```python
import jax
import jax.numpy as jnp
from jax import lax

D = 256
HEADS = 2
KEY = 128
FF = 1024
HID = 384
SLOTS = 512
CORE_LAYERS = 3
FEW = 20
GLEN = 8
FRAMES = 512


def game_orders(key):
    games = FRAMES // GLEN
    keys = jax.random.split(key, games)

    def shuffle(single):
        return jax.random.permutation(single, GLEN)
    return jax.vmap(shuffle)(keys).astype(jnp.int32)


def draw_order(key, part):
    shuffles = game_orders(key)
    games = FRAMES // GLEN
    source = (jnp.arange(games, dtype=jnp.int32) + games // 2) % games
    return (source[:, None] * GLEN + shuffles).reshape(FRAMES).astype(jnp.int32)


def draw_counts(key, part):
    shuffles = game_orders(key)
    key = jax.random.fold_in(key, 5)
    games = FRAMES // GLEN
    place = jnp.argsort(shuffles, axis=1).astype(jnp.int32)
    phase_key, level_key, high_key, low_key = jax.random.split(key, 4)
    phase = jax.random.randint(phase_key, (games, 1), 0, 3)
    along = jnp.roll(phase * (GLEN // 2) + place, games // 2, axis=0).reshape(FRAMES)
    level = jax.random.randint(level_key, (FRAMES,), 0, 65)
    early = FEW + (SLOTS // 2 - FEW) * level // 64
    late = SLOTS - (SLOTS - SLOTS // 4) * level * level * level // 262144
    amounts = jnp.where(along >= GLEN, late, early)
    fullest = jax.random.randint(high_key, (), 0, FRAMES)
    emptiest = (fullest + 1 + jax.random.randint(low_key, (), 0, FRAMES - 1)) % FRAMES
    return amounts.at[fullest].set(SLOTS).at[emptiest].set(FEW).astype(jnp.int32)


def levels(rng, shape, shards, low, largest):
    level, own = 1.0, jax.random.fold_in(rng, 6)
    for dim, blocks in shards:
        heights = jnp.exp(jax.random.uniform(jax.random.fold_in(own, dim), (blocks,), jnp.float32, low / len(shards), largest / len(shards)))
        level = level * jnp.repeat(heights, shape[dim] // blocks).reshape([-1 if axis == dim else 1 for axis in range(len(shape))])
    return level


def bell_draw(rng, shape, deviation, most, pieces=(), held_as=jnp.bfloat16):
    entries = jax.random.normal(rng, shape, jnp.float32) * deviation
    if len(pieces) > 0:
        entries = levels(rng, shape, pieces, -0.22, 0.18) * entries
    return jnp.clip(entries, min=-most, max=most).astype(held_as)


def setup_inputs(seed: int = 0) -> dict:
    key_list = jax.random.split(jax.random.key(seed), 20)
    entities = bell_draw(key_list[0], (FRAMES, SLOTS, D), 1.0, 6.0, ((0, 32),))
    counts = draw_counts(jax.random.fold_in(key_list[19], 71), 0)
    order = draw_order(jax.random.fold_in(key_list[19], 71), 0)
    first_gain = jnp.clip(1.0 + 0.1 * jax.random.normal(key_list[3], (D,), jnp.float32), 0.5, 1.5)
    first_shift = bell_draw(key_list[4], (D,), 0.3, 1.75, (), jnp.float32)
    attend_in = bell_draw(key_list[5], (D, 3 * HEADS * KEY), D ** -0.5, 0.375)
    attend_out = bell_draw(key_list[6], (HEADS * KEY, D), 0.5, 3.0)
    second_gain = jnp.clip(1.0 + 0.1 * jax.random.normal(key_list[7], (D,), jnp.float32), 0.5, 1.5)
    second_shift = bell_draw(key_list[8], (D,), 0.3, 1.75, (), jnp.float32)
    up_weight = bell_draw(key_list[9], (D, FF), D ** -0.5, 0.375)
    up_bias = bell_draw(key_list[10], (FF,), 0.5, 3.0, (), jnp.float32)
    down_weight = bell_draw(key_list[11], (FF, D), FF ** -0.5, 0.1875)
    down_bias = bell_draw(key_list[12], (D,), 0.3, 1.75, (), jnp.float32)
    core_input = bell_draw(key_list[13], (D, 4 * HID), 0.25, 1.5)
    core_upper = bell_draw(key_list[14], (CORE_LAYERS - 1, HID, 4 * HID), (2 * HID ** -0.5), 0.625)
    core_loop = bell_draw(key_list[15], (CORE_LAYERS, HID, 4 * HID), HID ** -0.5, 0.3125)
    core_first_bias = bell_draw(key_list[16], (4 * HID,), 0.5, 3.0, (), jnp.float32)
    core_upper_bias = bell_draw(key_list[17], (CORE_LAYERS - 1, 4 * HID), 0.5, 3.0, (), jnp.float32)
    core_grad = bell_draw(key_list[18], (FRAMES, HID), 1.0, 6.0, ((0, 32),))
    return {"entities": entities, "counts": counts, "order": order, "first_gain": first_gain, "first_shift": first_shift, "attend_in": attend_in, "attend_out": attend_out, "second_gain": second_gain, "second_shift": second_shift, "up_weight": up_weight, "up_bias": up_bias, "down_weight": down_weight, "down_bias": down_bias, "core_input": core_input, "core_upper": core_upper, "core_loop": core_loop, "core_first_bias": core_first_bias, "core_upper_bias": core_upper_bias, "core_grad": core_grad}


highest = lax.Precision.HIGHEST
epsilon = 1e-05
masked_score = -1e+30

@jax.custom_vjp
def low(v):
    return lax.optimization_barrier(v.astype(jnp.bfloat16)).astype(jnp.float32)

@jax.custom_vjp
def low_back(v):
    return v

def low_keep(v):
    return (low(v), None)

def low_pass(kept, grad):
    return (grad,)

def back_keep(v):
    return (v, None)

def back_low(kept, grad):
    return (low(grad),)
low.defvjp(low_keep, low_pass)
low_back.defvjp(back_keep, back_low)

def both_ways(values):
    return low_back(low(values))

def layer_norm(values, gain, shift):
    average = lax.optimization_barrier(jnp.mean(values, axis=-1, keepdims=True))
    centred = values - average
    variance = lax.optimization_barrier(jnp.mean(centred * centred, axis=-1, keepdims=True))
    return centred * lax.rsqrt(variance + epsilon) * gain + shift

def activate(values):
    return jax.nn.gelu(values, approximate=True)

def lstm_cell(gates, cell_prev):
    width = cell_prev.shape[-1]
    input_gate = jax.nn.sigmoid(gates[..., :width])
    forget_gate = jax.nn.sigmoid(gates[..., width:2 * width])
    candidate = jnp.tanh(gates[..., 2 * width:3 * width])
    output_gate = jax.nn.sigmoid(gates[..., 3 * width:])
    cell_next = forget_gate * cell_prev + input_gate * candidate
    return (cell_next, output_gate * jnp.tanh(cell_next))

def encode_group(frames, valid, encoder):
    first_gain, first_shift, attend_in, attend_out, second_gain, second_shift, up_weight, up_bias, down_weight, down_bias = encoder
    groups = frames.shape[0]
    normed = low(layer_norm(frames, first_gain, first_shift))
    mixed = both_ways(jnp.einsum('bsd,de->bse', normed, attend_in, precision=highest))
    mixed = mixed.reshape(groups, SLOTS, 3, HEADS, KEY)
    scores = jnp.einsum('bqhk,bthk->bhqt', mixed[:, :, 0], mixed[:, :, 1], precision=highest) * KEY ** (-0.5)
    scores = jnp.where(valid[:, None, None, :], low_back(scores), masked_score)
    weights = low(jax.nn.softmax(scores, axis=-1))
    attended = both_ways(jnp.einsum('bhqt,bthk->bqhk', weights, mixed[:, :, 2], precision=highest))
    attended = attended.reshape(groups, SLOTS, HEADS * KEY)
    middle = frames + low_back(jnp.einsum('bse,ed->bsd', attended, attend_out, precision=highest))
    normed_two = low(layer_norm(middle, second_gain, second_shift))
    hidden = low_back(jnp.einsum('bsd,df->bsf', normed_two, up_weight, precision=highest) + up_bias)
    activated = low(activate(hidden))
    final = middle + low_back(jnp.einsum('bsf,fd->bsd', activated, down_weight, precision=highest) + down_bias)
    present = lax.optimization_barrier(jnp.sum(valid, axis=1)).astype(jnp.float32)
    pooled = lax.optimization_barrier(jnp.sum(jnp.where(valid[:, :, None], final, 0.0), axis=1)) / present[:, None]
    return both_ways(pooled)

def run_core(sequences, core_input, core_upper, core_loop, core_first_bias, core_upper_bias):
    layer_input = sequences
    games = sequences.shape[0]
    for depth in range(CORE_LAYERS):
        weight = core_input if depth == 0 else core_upper[depth - 1]
        gate_bias = core_first_bias if depth == 0 else core_upper_bias[depth - 1]
        loop_weight = core_loop[depth]
        entering = jnp.einsum('gti,ij->tgj', layer_input, weight, precision=highest) + gate_bias

        def advance(carry, entering_step, loop_weight=loop_weight):
            state, cell = carry
            gates = entering_step + jnp.dot(state, loop_weight, precision=highest)
            cell_next, state_next = lstm_cell(gates, cell)
            return ((state_next, cell_next), state_next)
        start = (jnp.zeros((games, HID), jnp.float32), jnp.zeros((games, HID), jnp.float32))
        _, states = lax.scan(advance, start, entering)
        layer_input = jnp.swapaxes(states, 0, 1)
    return layer_input

def reference(entities, counts, order, first_gain, first_shift, attend_in, attend_out, second_gain, second_shift, up_weight, up_bias, down_weight, down_bias, core_input, core_upper, core_loop, core_first_bias, core_upper_bias, core_grad):
    valid = jnp.arange(SLOTS)[None, :] < counts[:, None]
    encoder = tuple((member.astype(jnp.float32) for member in (first_gain, first_shift, attend_in, attend_out, second_gain, second_shift, up_weight, up_bias, down_weight, down_bias)))
    core = tuple((member.astype(jnp.float32) for member in (core_input, core_upper, core_loop, core_first_bias, core_upper_bias)))

    def forward(frames, encoder_params, core_params):
        groups = frames.reshape(FRAMES // GLEN, GLEN, SLOTS, D)
        masks = valid.reshape(FRAMES // GLEN, GLEN, SLOTS)
        checked = jax.checkpoint(encode_group)

        def apply(items):
            return checked(items[0], items[1], encoder_params)
        pooled = lax.map(apply, (groups, masks)).reshape(FRAMES, D)
        sequences = pooled[order].reshape(FRAMES // GLEN, GLEN, D)
        return run_core(sequences, core_params[0], core_params[1], core_params[2], core_params[3], core_params[4]).reshape(FRAMES, HID)
    core_out, pull = jax.vjp(forward, entities.astype(jnp.float32), encoder, core)
    frames_back, encoder_back, core_back = pull(core_grad.astype(jnp.float32))
    return (core_out.astype(jnp.bfloat16), frames_back.astype(jnp.bfloat16), encoder_back[0], encoder_back[1], encoder_back[2], encoder_back[3], encoder_back[4], encoder_back[5], encoder_back[6], encoder_back[7], encoder_back[8], encoder_back[9], core_back[0], core_back[1], core_back[2], core_back[3], core_back[4])
```

```python
import functools

import jax
import jax.numpy as jnp
from jax import lax
from jax.experimental import pallas as pl
from jax.experimental.pallas import tpu as pltpu
from jax.sharding import PartitionSpec as P

HEADS = 2
KEY = 128
SLOTS = 512
GLEN = 8
WIDTH = 256
ROWS = 8
epsilon = 1e-05
bf16 = jnp.bfloat16
f32 = jnp.float32
MB = 1 << 20
KEY_SCALE = float(KEY ** -0.5)
EXP_SCALE = float(KEY ** -0.5 * 1.4426950408889634)
CG = 0.7978845608028654


def mm(a, b, ca=1, cb=0):
    return lax.dot_general(a, b, (((ca,), (cb,)), ((), ())), preferred_element_type=f32)


def whole(shape):
    return pl.BlockSpec(shape, lambda i, *_: (0,) * len(shape))


def skewed(items, *stages):
    held = {}
    for t in range(len(items) + len(stages) - 1):
        for k in range(len(stages)):
            i = t - k
            if 0 <= i < len(items):
                held[i] = stages[k](items[i], held.get(i))
    return [held[i] for i in range(len(items))]


def gelu_pair(v):
    c = lambda x: jnp.asarray(x, bf16)
    v2 = v * v
    s = 0.5 + 0.5 * jnp.tanh(v * (CG + (CG * 0.044715) * v2))
    g = (v * s).astype(bf16)
    s = s.astype(bf16)
    d = s + (g - g * s) * (c(2 * CG) + c(6 * CG * 0.044715) * v2.astype(bf16))
    return g, d


def colsum16(n, count, a):
    rows = lax.broadcasted_iota(jnp.int32, (n, 1), 0) < count
    a = jnp.where(rows, a, jnp.asarray(0, bf16))
    t = a[:128]
    for i in range(128, n, 128):
        t = t + a[i:i + 128]
    return jnp.sum(t.astype(f32), axis=0, keepdims=True)


def wide(r):
    return jnp.concatenate([r, r], axis=1)

def stage_mix(cfg, n, ents, g1, b1, w_in, centre, ones, outs, xcs):
    RC = (cfg['RC'] if n % cfg['RC'] == 0 else n)
    items = [(f, r) for r in range(0, n, RC) for f in range(len(ents))]
    def shift(it, _):
        f, r = it
        return mm(ents[f][0, r:r + RC, :], centre[...])
    def square(it, xc):
        f, r = it
        xcs[f][r:r + RC, :] = xc
        return jnp.mean(xc * xc, axis=1, keepdims=True)
    def norm(it, var):
        f, r = it
        scale = jnp.broadcast_to(lax.rsqrt(var + epsilon), (RC, 128))
        z1 = xcs[f][r:r + RC, :] * wide(scale)
        outs[f][0][0, r:r + RC, :] = z1.astype(bf16)
        outs[f][1][0, r:r + RC, :] = scale.astype(bf16)
        return (z1 * g1[...] + b1[...]).astype(bf16)
    def mix(it, normed):
        f, r = it
        qs = mm(normed, w_in[:, :256]) * EXP_SCALE
        outs[f][2][0, r:r + RC, :256] = qs.astype(bf16)
        outs[f][2][0, r:r + RC, 256:] = mm(normed, w_in[:, 256:]).astype(bf16)
    skewed(items, shift, square, norm, mix)

def stage_attention(cfg, n, counts_, outs):
    QC = (cfg['QC'] if n % cfg['QC'] == 0 else n)
    items = [(f, h, c) for h in range(HEADS) for c in range(0, n, QC) for f in range(len(outs))]
    vts, ks = {}, {}
    for f in range(len(outs)):
        for h in range(HEADS):
            vt = outs[f][2][0, :n, (2 * HEADS + h) * KEY:(2 * HEADS + h + 1) * KEY].T
            vt = jnp.concatenate([vt, jnp.ones((16, n), bf16)], axis=0)
            vts[f, h] = jnp.where(lax.broadcasted_iota(jnp.int32, (KEY + 16, n), 1) < counts_[f], vt, jnp.asarray(0, bf16))
            k = outs[f][2][0, :n, (HEADS + h) * KEY:(HEADS + h + 1) * KEY]
            ks[f, h] = jnp.where(lax.broadcasted_iota(jnp.int32, (n, 1), 0) < counts_[f], k, k[0:1])
    def score(it, _):
        f, h, c = it
        mixed_out = outs[f][2]
        q = mixed_out[0, c:c + QC, h * KEY:(h + 1) * KEY]
        return mm(ks[f, h], q, 1, 1)
    def soft(it, s):
        f, h, c = it
        largest = jnp.max(s, axis=0, keepdims=True)
        p = jnp.exp2(s - largest).astype(bf16)
        outs[f][3][0, h, :n, c:c + QC] = p
        return p
    def out(it, p):
        f, h, c = it
        att = mm(vts[f, h], p)
        linv = 1.0 / att[KEY:KEY + 1]
        outs[f][5][0, h:h + 1, c:c + QC] = linv
        outs[f][4][0, h * KEY:(h + 1) * KEY, c:c + QC] = (att[:KEY] * linv).astype(bf16)
    skewed(items, score, soft, out)

def stage_mid(cfg, n, counts_, ents, w_out, w_out_c, g2, b2, ones, outs, xcs, normeds, z2ts):
    RC = (cfg['RC'] if n % cfg['RC'] == 0 else n)
    items = [(f, r) for r in range(0, n, RC) for f in range(len(ents))]
    for f in range(len(ents)):
        rowsf = jnp.where(lax.broadcasted_iota(jnp.int32, (16, n), 1) < counts_[f], 1.0, 0.0).astype(bf16)
        z2ts[f][WIDTH:, :n] = rowsf
        outs[f][10][0, 0:1] = mm(rowsf, ents[f][0, :n, :])[0:1]
        outs[f][10][0, 1:2] = mm(rowsf, outs[f][4][0, :, :n], 1, 1)[0:1]
    def proj(it, _):
        f, r = it
        att = outs[f][4][0, :, r:r + RC].T
        average = mm(att, w_out_c[...])
        return mm(att, w_out[...]) - wide(average[:, :128] + average[:, 128:]) + xcs[f][r:r + RC, :]
    def square(it, mc):
        return mc, jnp.mean(mc * mc, axis=1, keepdims=True)
    def norm(it, held):
        f, r = it
        mc, var = held
        scale = jnp.broadcast_to(lax.rsqrt(var + epsilon), (RC, 128))
        outs[f][7][0, r:r + RC, :] = scale.astype(bf16)
        z2 = mc * wide(scale)
        normeds[f][r:r + RC, :] = (z2 * g2[...] + b2[...]).astype(bf16)
        z2 = z2.astype(bf16)
        outs[f][6][0, r:r + RC, :] = z2
        rows = lax.broadcasted_iota(jnp.int32, (RC, 1), 0) + r < counts_[f]
        z2ts[f][:WIDTH, r:r + RC] = jnp.where(rows, z2, jnp.asarray(0, bf16)).T
    skewed(items, proj, square, norm)

def stage_ffn(cfg, n, counts_, normeds, z2ts, w_up, up_bias, outs):
    CH = cfg['CH']
    items = [(f, c) for c in range(0, w_up.shape[1], CH) for f in range(len(outs))]
    def up(it, _):
        f, c = it
        return mm(normeds[f][:n, :], w_up[:, c:c + CH])
    def act(it, v):
        f, c = it
        g, d = gelu_pair(v + up_bias[:, c:c + CH])
        outs[f][8][0, :n, c:c + CH] = d
        outs[f][11][0, :, c:c + CH] = colsum16(n, counts_[f], g)
        return d
    def grad(it, d):
        f, c = it
        m = mm(z2ts[f][:, :n], d)
        outs[f][9][0, :, c:c + CH] = m[:WIDTH].astype(bf16)
        outs[f][12][0, :, c:c + CH] = m[WIDTH:WIDTH + 1]
    skewed(items, up, act, grad)

FORWARD = dict(QC=512, RC=256, CH=256, F=2, parts=('mix','att','mid','ffn'))

def frame_all(cfg, n, counts_, ents, weights, outs, scratch):
    g1, b1, w_in, w_out, g2, b2, w_up, up_bias = weights
    centre, ones, w_out_c, xc, normed, z2t = scratch
    F = len(ents)
    xcs = [xc.at[f] for f in range(F)]
    normeds = [normed.at[f] for f in range(F)]
    z2ts = [z2t.at[f] for f in range(F)]
    parts = cfg['parts']
    if 'mix' in parts: stage_mix(cfg, n, ents, g1, b1, w_in, centre, ones, outs, xcs)
    if 'att' in parts: stage_attention(cfg, n, counts_, outs)
    if 'mid' in parts: stage_mid(cfg, n, counts_, ents, w_out, w_out_c, g2, b2, ones, outs, xcs, normeds, z2ts)
    if 'ffn' in parts: stage_ffn(cfg, n, counts_, normeds, z2ts, w_up, up_bias, outs)

def forward_kernel(cfg, counts, ent, g1, b1, w_in, w_out, g2, b2, w_up, up_bias, *rest):
    outs, scratch = rest[:13], rest[13:]
    F = cfg['F']
    step = pl.program_id(0)
    @pl.when(step == 0)
    def _():
        centre, ones, w_out_c = scratch[:3]
        same = lax.broadcasted_iota(jnp.int32, (WIDTH, WIDTH), 0) == lax.broadcasted_iota(jnp.int32, (WIDTH, WIDTH), 1)
        centre[...] = (jnp.where(same, 1.0, 0.0) - 1.0 / WIDTH).astype(bf16)
        ones[...] = jnp.full(ones.shape, 1.0 / WIDTH, bf16)
        average = jnp.broadcast_to(jnp.mean(w_out[...].astype(f32), axis=1, keepdims=True), (WIDTH, 128))
        high = average.astype(bf16)
        w_out_c[...] = jnp.concatenate([high, (average - high.astype(f32)).astype(bf16)], axis=1)
    cs = [counts[step * F + i] for i in range(F)]
    most = functools.reduce(jnp.maximum, cs)
    blocks = (most + 127) // 128
    for b in range(1, SLOTS // 128 + 1):
        @pl.when(blocks == b)
        def _(b=b):
            frame_all(cfg, b * 128, cs, [ent.at[pl.ds(i, 1)] for i in range(F)], (g1, b1, w_in, w_out, g2, b2, w_up, up_bias),
                      [[o.at[pl.ds(i, 1)] for o in outs] for i in range(F)], scratch)

def run_forward(entities, counts, g1, b1, w_in, w_out, g2, b2, w_up, up_bias, const=False):
    cfg = FORWARD
    frames = entities.shape[0]
    ff = w_up.shape[1]
    F = cfg['F']
    def per_frame(shape):
        return pl.BlockSpec((F,) + shape, lambda i, *_: ((0 if const else i),) + (0,) * len(shape))
    outs = [((SLOTS, WIDTH), bf16), ((SLOTS, 128), bf16), ((SLOTS, 768), bf16), ((HEADS, SLOTS, SLOTS), bf16),
            ((HEADS * KEY, SLOTS), bf16), ((HEADS, SLOTS), f32), ((SLOTS, WIDTH), bf16), ((SLOTS, 128), bf16), ((SLOTS, ff), bf16),
            ((WIDTH, ff), bf16), ((2, WIDTH), f32), ((1, ff), f32), ((1, ff), f32)]
    return pl.pallas_call(
        functools.partial(forward_kernel, cfg),
        grid_spec=pltpu.PrefetchScalarGridSpec(
            num_scalar_prefetch=1, grid=(frames // F,),
            in_specs=[per_frame((SLOTS, WIDTH))] + [whole(a.shape) for a in (g1, b1, w_in, w_out, g2, b2, w_up, up_bias)],
            out_specs=[per_frame(s) for s, _ in outs],
            scratch_shapes=[pltpu.VMEM((WIDTH, WIDTH), bf16), pltpu.VMEM((WIDTH, 128), bf16), pltpu.VMEM((WIDTH, WIDTH), bf16),
                            pltpu.VMEM((F, SLOTS, WIDTH), f32), pltpu.VMEM((F, SLOTS, WIDTH), bf16), pltpu.VMEM((F, WIDTH + 16, SLOTS), bf16)]),
        out_shape=[jax.ShapeDtypeStruct((frames,) + s, d) for s, d in outs],
        compiler_params=pltpu.CompilerParams(vmem_limit_bytes=60 * MB),
        name="encode_forward",
    )(counts, entities, g1, b1, w_in, w_out, g2, b2, w_up, up_bias)


BACKWARD = dict(QC=256, RC=256, F=2, parts=('ffn', 'att', 'mix'))

def frame_back(cfg, n, counts_, rows_, ents, weights, fr, outs, scratch):
    F = len(counts_)
    spread, scale, g_unused, w_out = weights
    entity_grad, g_sum, in_sum, out_sum, mix_sum = outs
    upc, winc, ones, mids, ds, mixed_back, z1t, ub = scratch
    z1s, r1s, mixeds, probs, atts, linvs, z2s, r2s, dacts, ms = fr
    parts = cfg['parts']
    RC = (cfg['RC'] if n % cfg['RC'] == 0 else n)
    QC = (cfg['QC'] if n % cfg['QC'] == 0 else n)
    dots, inners = {}, {}
    bbs = {}
    if 'ffn' in parts:
        for f in range(F):
            a = scale[rows_[f]]
            ub[f] = (upc[...] * a).astype(bf16)
            g_sum[...] += ms[f][0].astype(f32) * a
        items = [(f, r) for r in range(0, n, RC) for f in range(F)]
        def up(it, _):
            f, r = it
            return mm(dacts[f][0, r:r + RC, :], ub[f], 1, 1)
        def dot(it, uc):
            f, r = it
            return uc, mm((uc * z2s[f][0, r:r + RC, :].astype(f32)).astype(bf16), ones[...])
        def mid(it, held):
            f, r = it
            uc, d = held
            r2 = r2s[f][0, r:r + RC, :].astype(f32)
            back = wide(r2) * (uc - z2s[f][0, r:r + RC, :].astype(f32) * wide(d)) + spread[rows_[f]]
            rows = lax.broadcasted_iota(jnp.int32, (RC, 1), 0) + r < counts_[f]
            back = jnp.where(rows, back, 0.0)
            mids[f, r:r + RC, :] = back
            return back.astype(bf16)
        low = dict(zip(items, skewed(items, up, dot, mid)))
        for f in range(F):
            bb = jnp.concatenate([low[f, r] for r in range(0, n, RC)], axis=0)
            bbs[f] = bb
        out_sum[...] += functools.reduce(jnp.add, [mm(atts[f][0, :, :n], bbs[f]) for f in range(F)])
    if 'att' in parts:
        for f in range(F):
            do = mm(w_out[...], bbs[f], 1, 1) if 'ffn' in parts else atts[f][0, :, :n].astype(f32)
            for h in range(HEADS):
                d = do[h * KEY:(h + 1) * KEY] * linvs[f][0, h:h + 1, :n]
                inners[f, h] = jnp.sum(d * atts[f][0, h * KEY:(h + 1) * KEY, :n].astype(f32), axis=0, keepdims=True)
                dots[f, h] = d.astype(bf16)
        items = [(f, h, c) for h in range(HEADS) for c in range(0, n, QC) for f in range(F)]
        def prob(it, _):
            f, h, c = it
            v = mixeds[f][0, :n, (2 * HEADS + h) * KEY:(2 * HEADS + h + 1) * KEY]
            return mm(v, dots[f, h][:, c:c + QC])
        def score(it, dp):
            f, h, c = it
            ds[f, h, :n, c:c + QC] = probs[f][0, h, :n, c:c + QC] * (dp - inners[f, h][:, c:c + QC]).astype(bf16)
        def finish(it, _):
            f, h, c = it
            if c + QC < n:
                return
            lo = f * n
            q = mixeds[f][0, :n, h * KEY:(h + 1) * KEY]
            rows = lax.broadcasted_iota(jnp.int32, (n, 1), 0) < counts_[f]
            k = jnp.where(rows, mixeds[f][0, :n, (HEADS + h) * KEY:(HEADS + h + 1) * KEY], jnp.asarray(0, bf16))
            d = ds[f, h, :n, :n]
            kb = jnp.where(rows, mm(d, q) * (KEY_SCALE / EXP_SCALE), 0.0)
            mixed_back[lo:lo + n, (HEADS + h) * KEY:(HEADS + h + 1) * KEY] = kb.astype(bf16)
            vb = jnp.where(rows, mm(probs[f][0, h, :n, :n], dots[f, h], 1, 1), 0.0)
            mixed_back[lo:lo + n, (2 * HEADS + h) * KEY:(2 * HEADS + h + 1) * KEY] = vb.astype(bf16)
            qt = (mm(k, d, 0, 0) * KEY_SCALE).astype(bf16)
            mixed_back[lo:lo + n, h * KEY:(h + 1) * KEY] = qt.T
        skewed(items, prob, score, finish)
    if 'mix' in parts:
        for f in range(F):
            z1t[:WIDTH, f * n:(f + 1) * n] = z1s[f][0, :n, :].T
        z1t[WIDTH:, :F * n] = jnp.ones((16, F * n), bf16)
        for c in range(0, 768, 256):
            grad = mm(z1t[:, :F * n], mixed_back[:F * n, c:c + 256])
            in_sum[:, c:c + 256] += grad[:WIDTH]
            mix_sum[:, c:c + 256] += grad[WIDTH:WIDTH + 1]
        items = [(f, r) for r in range(0, n, RC) for f in range(F)]
        def back1(it, _):
            f, r = it
            return mm(mixed_back[f * n + r:f * n + r + RC, :], winc[...], 1, 1)
        def dot1(it, uc):
            f, r = it
            return uc, mm((uc * z1s[f][0, r:r + RC, :].astype(f32)).astype(bf16), ones[...])
        def last1(it, held):
            f, r = it
            uc, d = held
            r1 = r1s[f][0, r:r + RC, :].astype(f32)
            eg = mids[f, r:r + RC, :] + wide(r1) * (uc - z1s[f][0, r:r + RC, :].astype(f32) * wide(d))
            entity_grad[f, r:r + RC, :] = eg.astype(bf16)
        skewed(items, back1, dot1, last1)
        if n < SLOTS:
            for f in range(F):
                entity_grad[f, n:, :] = jnp.zeros((SLOTS - n, WIDTH), bf16)

def backward_kernel(cfg, counts, spread, scale, g1, w_in, w_out, g2, w_up, *rest):
    fr, outs, scratch = rest[:10], rest[10:15], rest[15:]
    F = cfg['F']
    step = pl.program_id(0)
    entity_grad, g_sum, in_sum, out_sum, mix_sum = outs
    upc, winc, ones = scratch[:3]
    @pl.when(step == 0)
    def _():
        w = g2[...] * w_up[...].astype(f32)
        upc[...] = w - jnp.mean(w, axis=0, keepdims=True)
        w = g1[...] * w_in[...].astype(f32)
        winc[...] = (w - jnp.mean(w, axis=0, keepdims=True)).astype(bf16)
        ones[...] = jnp.full(ones.shape, 1.0 / WIDTH, bf16)
        for o in outs[1:]:
            o[...] = jnp.zeros(o.shape, f32)
    cs = [counts[step * F + i] for i in range(F)]
    most = functools.reduce(jnp.maximum, cs)
    blocks = (most + 127) // 128
    for b in range(1, SLOTS // 128 + 1):
        @pl.when(blocks == b)
        def _(b=b):
            frame_back(cfg, b * 128, cs, [pl.ds(i, 1) for i in range(F)], None, (spread.at[0], scale.at[0], None, w_out),
                       [[o.at[pl.ds(i, 1)] for i in range(F)] for o in fr], outs, scratch)

def run_backward(counts, spread, scale, g1c, w_in, w_out, g2c, w_up, kept):
    cfg = BACKWARD
    frames = spread.shape[0]
    ff = w_up.shape[1]
    F = cfg['F']
    def per_frame(shape):
        return pl.BlockSpec((F,) + shape, lambda i, *_: (i,) + (0,) * len(shape))
    acc = [(WIDTH, ff), (WIDTH, 768), (WIDTH, WIDTH), (1, 768)]
    spread = spread.reshape(frames // F, F, WIDTH)
    scale = scale.reshape(frames // F, F, ff)
    return pl.pallas_call(
        functools.partial(backward_kernel, cfg),
        grid_spec=pltpu.PrefetchScalarGridSpec(
            num_scalar_prefetch=1, grid=(frames // F,),
            in_specs=[pl.BlockSpec((1, F, WIDTH), lambda i, *_: (i, 0, 0)), pl.BlockSpec((1, F, ff), lambda i, *_: (i, 0, 0))]
            + [whole(a.shape) for a in (g1c, w_in, w_out, g2c, w_up)] + [per_frame(a.shape[1:]) for a in kept],
            out_specs=[per_frame((SLOTS, WIDTH))] + [whole(s) for s in acc],
            scratch_shapes=[pltpu.VMEM((WIDTH, ff), f32), pltpu.VMEM((WIDTH, 768), bf16), pltpu.VMEM((WIDTH, 128), bf16),
                            pltpu.VMEM((F, SLOTS, WIDTH), f32), pltpu.VMEM((F, HEADS, SLOTS, SLOTS), bf16), pltpu.VMEM((F * SLOTS, 768), bf16),
                            pltpu.VMEM((WIDTH + 16, F * SLOTS), bf16), pltpu.VMEM((F, WIDTH, ff), bf16)]),
        out_shape=[jax.ShapeDtypeStruct((frames, SLOTS, WIDTH), bf16)] + [jax.ShapeDtypeStruct(s, f32) for s in acc],
        compiler_params=pltpu.CompilerParams(vmem_limit_bytes=60 * MB),
        name="encode_backward",
    )(counts, spread, scale, g1c, w_in, w_out, g2c, w_up, *kept)


def halves(a):
    high = a.astype(bf16)
    return high, (a - high.astype(f32)).astype(bf16)

def mm_wide(a, w, cb=0):
    high, rest = halves(a)
    both = mm(jnp.concatenate([high, rest], axis=0), w, 1, cb)
    return both[:a.shape[0]] + both[a.shape[0]:]

def core_kernel(counts, sums, acts, dsums, packed, w_out, down, down_bias, w_in, w_upper, w_loop, first_bias, upper_bias,
                core_out, spread_out, scale_out, factors, rest, small_out, loop_t, gates_keep, cell_keep):
    frames = sums.shape[0]
    games = frames // GLEN
    hid = w_loop.shape[1]
    depth = w_loop.shape[0]
    total = GLEN * ROWS
    wide_gates = 4 * hid
    for l in range(depth):
        loop_t[l] = w_loop[l].T
    present = counts[...].astype(f32)
    numer = sums[:, 0, :] + mm_wide(sums[:, 1, :], w_out[...]) + mm_wide(acts[:, 0, :], down[...])
    pooled = (numer / present + down_bias[...]).astype(bf16)
    row = lax.broadcasted_iota(jnp.int32, (total, frames), 0)
    col = lax.broadcasted_iota(jnp.int32, (total, frames), 1)
    spot = (col // GLEN == row % ROWS) & (col % GLEN == row // ROWS)
    spot = jnp.where(spot, 1.0, 0.0).astype(bf16)
    places = packed[:, hid:hid + frames].astype(f32)
    frame = lax.broadcasted_iota(jnp.int32, (frames, frames), 1).astype(f32)
    pick = jnp.where(places == frame, 1.0, 0.0).astype(bf16)
    pick = mm(spot, pick).astype(bf16)
    x = mm(pick, pooled)
    xs, prevs = [x], []
    for l in range(depth):
        w = w_in[...] if l == 0 else w_upper[l - 1]
        bias = first_bias[...] if l == 0 else upper_bias[l - 1:l, :]
        entering = (mm(x.astype(bf16), w) if l == 0 else mm_wide(x, w)) + bias
        state = jnp.zeros((ROWS, hid), f32)
        cell = jnp.zeros((ROWS, hid), f32)
        states = []
        for t in range(GLEN):
            gates = entering[t * ROWS:(t + 1) * ROWS]
            if t > 0:
                gates = gates + mm_wide(state, w_loop[l])
            i = 0.5 + 0.5 * jnp.tanh(0.5 * gates[:, :hid])
            f = 0.5 + 0.5 * jnp.tanh(0.5 * gates[:, hid:2 * hid])
            g = jnp.tanh(gates[:, 2 * hid:3 * hid])
            o = 0.5 + 0.5 * jnp.tanh(0.5 * gates[:, 3 * hid:])
            cell_keep[l, t, 0] = cell
            cell = f * cell + i * g
            squashed = jnp.tanh(cell)
            cell_keep[l, t, 1] = squashed
            state = o * squashed
            states.append(state)
            gates_keep[l, t] = jnp.concatenate([i, f, g, o], axis=1)
        x = jnp.concatenate(states, axis=0)
        xs.append(x)
    unspot = lambda a: mm(spot, a.astype(bf16), 0, 0).astype(bf16)
    core_out[...] = unspot(xs[depth])
    at = 0
    for a in xs:
        rest[:, at:at + a.shape[1]] = unspot(a)
        at += a.shape[1]
    back = mm(spot, packed[:, :hid])
    for l in reversed(range(depth)):
        carried = jnp.zeros((ROWS, hid), f32)
        cell_carry = jnp.zeros((ROWS, hid), f32)
        gate_backs = [None] * GLEN
        for t in reversed(range(GLEN)):
            kept = gates_keep[l, t]
            i, f, g, o = [kept[:, k * hid:(k + 1) * hid] for k in range(4)]
            before, squashed = cell_keep[l, t, 0], cell_keep[l, t, 1]
            state_back = back[t * ROWS:(t + 1) * ROWS] + carried
            cell_back = state_back * (o * (1.0 - squashed * squashed)) + cell_carry
            gate_back = jnp.concatenate([cell_back * (g * i * (1.0 - i)), cell_back * (before * f * (1.0 - f)),
                                         cell_back * (i * (1.0 - g * g)), state_back * (squashed * o * (1.0 - o))], axis=1)
            cell_carry = cell_back * f
            if t > 0:
                carried = mm_wide(gate_back, loop_t[l])
            gate_backs[t] = gate_back
        gate_all = jnp.concatenate(gate_backs, axis=0)
        start = l * wide_gates
        factors[:, start:start + wide_gates] = unspot(gate_all)
        back = mm_wide(gate_all, w_in[...] if l == 0 else w_upper[l - 1], 1)
    pooled_back = mm(pick, back.astype(bf16), 0, 0)
    spread = pooled_back / present
    spread_out[...] = spread
    low = spread.astype(bf16)
    scale = mm(low, down[...], 1, 1)
    scale_out[...] = scale
    start = at
    ff = down.shape[0]
    rest[:, start:start + ff] = acts[:, 0, :].astype(bf16)
    rest[:, start + ff:] = low
    small_out[:, :ff] = jnp.sum(scale * dsums[:, 0, :], axis=0, keepdims=True)
    small_out[:, ff:] = jnp.sum(low.astype(f32) * present, axis=0, keepdims=True)

def run_core(counts, sums, acts, dsums, packed, w_out, down, down_bias, w_in, w_upper, w_loop, first_bias, upper_bias):
    frames = sums.shape[0]
    depth, hid, wide_gates = w_loop.shape
    ff, width = down.shape
    cols = width + depth * hid + ff + width
    return pl.pallas_call(
        core_kernel,
        out_shape=[jax.ShapeDtypeStruct((frames, hid), bf16), jax.ShapeDtypeStruct((frames, width), f32), jax.ShapeDtypeStruct((frames, ff), f32),
                   jax.ShapeDtypeStruct((frames, depth * wide_gates), bf16), jax.ShapeDtypeStruct((frames, cols), bf16), jax.ShapeDtypeStruct((1, ff + width), f32)],
        scratch_shapes=[pltpu.VMEM((depth, wide_gates, hid), bf16), pltpu.VMEM((depth, GLEN, ROWS, wide_gates), f32),
                        pltpu.VMEM((depth, GLEN, 2, ROWS, hid), f32)],
        compiler_params=pltpu.CompilerParams(vmem_limit_bytes=56 * MB),
        name="core",
    )(counts, sums, acts, dsums, packed, w_out, down, down_bias, w_in, w_upper, w_loop, first_bias, upper_bias)


MESH = pl.DeviceIdType.MESH


def ring_place(low):
    return low ^ (low // 2)


def remote(src, dst, sems, at, pipe, dp):
    return pltpu.make_async_remote_copy(src_ref=src, dst_ref=dst, send_sem=sems[0].at[at], recv_sem=sems[1].at[at],
                                        device_id=(pipe, dp), device_id_type=MESH)


class Gather:
    def __init__(self, own, out, up, down, ahead, behind, far, over, keep):
        self.own, self.out = own, out
        self.up, self.down, self.ahead, self.behind, self.far, self.over, self.keep = up, down, ahead, behind, far, over, keep
        self.n = lax.axis_size("dp")
        self.lines = self.n // 4
        self.pipe, self.dp = lax.axis_index("pipe"), lax.axis_index("dp")
        self.z, low = self.dp // 4, self.dp % 4
        place = ring_place(low)
        spot = lambda p: ring_place(p % 4)
        self.next = spot(place + 1)
        self.prev = spot(place + 3)
        self.diag = spot(place + 2)
        self.low = low
        self.rows = own.shape[0]
        self.pending = []

    def block(self, pipe, dp):
        return self.out.at[pl.ds(pl.multiple_of((pipe * self.n + dp) * self.rows, 16), self.rows), :]

    def send(self, src, dp, sems, at, pipe, to):
        copy = remote(src, self.block(self.pipe, dp), sems, at, pipe, to)
        copy.start()
        return copy

    def spread(self, src, z, at):
        dp = z * 4 + self.low
        here = self.z * 4
        self.send(src, dp, self.ahead, at, self.pipe, here + self.next)
        self.send(src, dp, self.behind, at, self.pipe, here + self.prev)
        self.send(src, dp, self.over, at, 1 - self.pipe, self.dp)

    def begin(self):
        self.local = pltpu.make_async_copy(self.own, self.block(self.pipe, self.dp), self.keep)
        self.local.start()
        @pl.when(self.z + 1 < self.lines)
        def _():
            self.send(self.own, self.dp, self.up, 0, self.pipe, self.dp + 4)
        @pl.when(self.z > 0)
        def _():
            self.send(self.own, self.dp, self.down, 0, self.pipe, self.dp - 4)
        self.spread(self.own, self.z, 0)

    def wait(self, sems, at, z, low, sent):
        block = self.block(self.pipe, z * 4 + low)
        copy = remote(block, block, sems, at, self.pipe, self.dp)
        copy.wait_send() if sent else copy.wait_recv()

    def present(self, s, side):
        z = self.z - s if side == 0 else self.z + s
        return z, (z >= 0 if side == 0 else z < self.lines)

    def line_step(self, s):
        for side, sems, other in ((0, self.up, 4), (1, self.down, -4)):
            z, there = self.present(s, side)
            at = 2 * s - 1 + side
            @pl.when(there)
            def _(z=z, at=at, sems=sems, other=other, side=side):
                self.wait(sems, s - 1, z, self.low, False)
                block = self.block(self.pipe, z * 4 + self.low)
                ahead = self.z + 1 < self.lines if side == 0 else self.z > 0
                @pl.when(ahead)
                def _():
                    self.send(block, z * 4 + self.low, sems, s, self.pipe, self.dp + other)
                self.spread(block, z, at)

    def slots(self, s):
        return [(0, self.z, None)] if s == 0 else [(2 * s - 1 + side,) + self.present(s, side) for side in (0, 1)]

    def ring_step(self, s):
        for at, z, there in self.slots(s):
            def go(at=at, z=z):
                here = self.z * 4
                count = 2 * self.lines
                self.wait(self.ahead, at, z, self.prev, False)
                block = self.block(self.pipe, z * 4 + self.prev)
                if at % 2 == 0:
                    self.send(block, z * 4 + self.prev, self.far, at, self.pipe, here + self.next)
                self.send(block, z * 4 + self.prev, self.over, count + at, 1 - self.pipe, self.dp)
                self.wait(self.behind, at, z, self.next, False)
                block = self.block(self.pipe, z * 4 + self.next)
                if at % 2 == 1:
                    self.send(block, z * 4 + self.next, self.far, at, self.pipe, here + self.prev)
                self.send(block, z * 4 + self.next, self.over, 2 * count + at, 1 - self.pipe, self.dp)
            go() if there is None else pl.when(there)(go)

    def far_step(self, s):
        for at, z, there in self.slots(s):
            def go(at=at, z=z):
                self.wait(self.far, at, z, self.diag, False)
                self.send(self.block(self.pipe, z * 4 + self.diag), z * 4 + self.diag, self.over, 6 * self.lines + at, 1 - self.pipe, self.dp)
            go() if there is None else pl.when(there)(go)

    def finish(self):
        count = 2 * self.lines
        self.local.wait()
        other = 1 - self.pipe
        @pl.when(self.z + 1 < self.lines)
        def _():
            self.wait(self.up, 0, self.z, self.low, True)
        @pl.when(self.z > 0)
        def _():
            self.wait(self.down, 0, self.z, self.low, True)
        for s in range(self.lines):
            for at, z, there in self.slots(s):
                def go(at=at, z=z):
                    for group, low in enumerate((self.low, self.prev, self.next, self.diag)):
                        block = self.block(other, z * 4 + low)
                        remote(block, block, self.over, group * count + at, self.pipe, self.dp).wait()
                    self.wait(self.ahead, at, z, self.low, True)
                    self.wait(self.behind, at, z, self.low, True)
                    self.wait(self.far, at, z, self.prev if at % 2 == 0 else self.next, True)
                go() if there is None else pl.when(there)(go)
            if s > 0:
                for side, sems in ((0, self.up), (1, self.down)):
                    z, there = self.present(s, side)
                    ahead = self.z + 1 < self.lines if side == 0 else self.z > 0
                    @pl.when(there & ahead)
                    def _(z=z, sems=sems):
                        self.wait(sems, s, z, self.low, True)

    def run(self):
        self.begin()
        for s in range(self.lines):
            if s > 0:
                self.line_step(s)
            if s > 0:
                self.ring_step(s - 1)
            if s > 1:
                self.far_step(s - 2)
        self.ring_step(self.lines - 1)
        for s in range(max(self.lines - 2, 0), self.lines):
            self.far_step(s)
        self.finish()


def gather_semaphores(devices):
    lines = devices // 2 // 4
    pair = lambda n: [pltpu.SemaphoreType.DMA((n,)), pltpu.SemaphoreType.DMA((n,))]
    return pair(lines) + pair(lines) + pair(2 * lines) + pair(2 * lines) + pair(2 * lines) + pair(8 * lines) + [pltpu.SemaphoreType.DMA]


def make_gather(own, out, sems):
    p = [tuple(sems[2 * i:2 * i + 2]) for i in range(6)]
    return Gather(own, out, *p, sems[12])


def greet():
    n = lax.axis_size("dp")
    pipe, dp = lax.axis_index("pipe"), lax.axis_index("dp")
    barrier = pltpu.get_barrier_semaphore()
    for k in range(n):
        to = lax.rem(dp + k, n)
        pl.semaphore_signal(barrier, inc=1, device_id=(1 - pipe, to), device_id_type=MESH)
        if k > 0:
            pl.semaphore_signal(barrier, inc=1, device_id=(pipe, to), device_id_type=MESH)
    pl.semaphore_wait(barrier, 2 * n - 1)


def exchange_kernel(gates, rest, g_sum, in_sum, out_sum, vec, core_out, gates_all, rest_all, sums_all, vec_all, core_all,
                    *scratch):
    sems = gather_semaphores(2 * lax.axis_size("dp"))
    k = len(sems)
    first, second = scratch[:k], scratch[k:2 * k]
    big, half, parts, pair_s, pair_r, rs_s, rs_r, ag_s, ag_r, vec_s, vec_r, keep = scratch[2 * k:]
    n = lax.axis_size("dp")
    pipe, dp = lax.axis_index("pipe"), lax.axis_index("dp")
    rows = big.shape[0]
    mid = rows // 2
    piece = mid // n
    greet()
    pair = lambda src, dst, at: pltpu.make_async_remote_copy(src_ref=src, dst_ref=dst, send_sem=pair_s.at[at], recv_sem=pair_r.at[at],
                                                             device_id=(1 - pipe, dp), device_id_type=MESH)
    for c in range(4):
        big[c * 256:(c + 1) * 256, :] = g_sum[:, c * 256:(c + 1) * 256].astype(bf16)
    for c in range(3):
        big[(4 + c) * 256:(5 + c) * 256, :] = in_sum[:, c * 256:(c + 1) * 256].astype(bf16)
    big[7 * 256:, :] = out_sum[...].astype(bf16)
    mine = pl.ds(pl.multiple_of(pipe * mid, 256), mid)
    theirs = pl.ds(pl.multiple_of((1 - pipe) * mid, 256), mid)
    first_pair = pair(big.at[theirs, :], half, 0)
    first_pair.start()
    swap = pair(core_out, core_all, 1)
    swap.start()
    ga = make_gather(gates, gates_all, first)
    re = make_gather(rest, rest_all, second)
    re.begin()
    ga.begin()
    tails = []
    own_slot = pl.ds(pl.multiple_of((pipe * n + dp) * 16, 16), 16)
    tail_keep = pltpu.make_async_copy(vec, vec_all.at[own_slot, :], keep.at[0])
    tail_keep.start()
    for j in range(1, 2 * n):
        side, step = j // n, j % n
        copy = pltpu.make_async_remote_copy(src_ref=vec, dst_ref=vec_all.at[own_slot, :], send_sem=vec_s.at[j], recv_sem=vec_r.at[j],
                                            device_id=((pipe + side) % 2, lax.rem(dp + step, n)), device_id_type=MESH)
        copy.start()
        tails.append(copy)
    first_pair.wait()
    big[mine, :] = (big[mine, :].astype(f32) + half[...].astype(f32)).astype(bf16)
    def cut(owner):
        return pl.ds(pl.multiple_of(pipe * mid + owner * piece, 16), piece)
    sends = []
    for j in range(1, n):
        to = lax.rem(dp + j, n)
        copy = pltpu.make_async_remote_copy(src_ref=big.at[cut(to), :], dst_ref=parts.at[j], send_sem=rs_s.at[j], recv_sem=rs_r.at[j],
                                            device_id=(pipe, to), device_id_type=MESH)
        copy.start()
        sends.append(copy)
    lines = n // 4
    for g in (re, ga):
        if lines > 1:
            g.line_step(1)
        g.ring_step(0)
    total = big[cut(dp), :].astype(f32)
    for j in range(1, n):
        sends[j - 1].wait_recv()
        total = total + parts[j].astype(f32)
    for copy in sends:
        copy.wait_send()
    sums_all[cut(dp), :] = total.astype(bf16)
    sends = []
    for j in range(1, n):
        to = lax.rem(dp + j, n)
        copy = pltpu.make_async_remote_copy(src_ref=sums_all.at[cut(dp), :], dst_ref=sums_all.at[cut(dp), :], send_sem=ag_s.at[j],
                                            recv_sem=ag_r.at[j], device_id=(pipe, to), device_id_type=MESH)
        copy.start()
        sends.append(copy)
    for s in range(2, lines):
        for g in (re, ga):
            g.line_step(s)
            g.ring_step(s - 1)
            g.far_step(s - 2)
    for g in (re, ga):
        if lines > 1:
            g.ring_step(lines - 1)
    for j in range(1, n):
        sends[j - 1].wait_send()
        source = lax.rem(dp + n - j, n)
        pltpu.make_async_remote_copy(src_ref=sums_all.at[cut(source), :], dst_ref=sums_all.at[cut(source), :], send_sem=ag_s.at[j],
                                     recv_sem=ag_r.at[j], device_id=(pipe, source), device_id_type=MESH).wait_recv()
    last = pair(sums_all.at[mine, :], sums_all.at[mine, :], 2)
    last.start()
    for s in range(max(lines - 2, 0), lines):
        for g in (re, ga):
            g.far_step(s)
    for g in (re, ga):
        g.finish()
    last.wait_send()
    pair(sums_all.at[theirs, :], sums_all.at[theirs, :], 2).wait_recv()
    swap.wait()
    tail_keep.wait()
    for j in range(1, 2 * n):
        side, step = j // n, j % n
        tails[j - 1].wait_send()
        slot = pl.ds(pl.multiple_of((lax.rem(pipe + side, 2) * n + lax.rem(dp + n - step, n)) * 16, 16), 16)
        pltpu.make_async_remote_copy(src_ref=vec, dst_ref=vec_all.at[slot, :], send_sem=vec_s.at[j], recv_sem=vec_r.at[j],
                                     device_id=(pipe, dp), device_id_type=MESH).wait_recv()


def run_exchange(gates, rest, g_sum, in_sum, out_sum, vec, core_out):
    n = lax.axis_size("dp")
    devices = 2 * n
    frames = gates.shape[0]
    rows = 2048
    anywhere = pl.BlockSpec(memory_space=pl.ANY)
    near = pl.BlockSpec(memory_space=pltpu.VMEM)
    dma = lambda m: pltpu.SemaphoreType.DMA((m,))
    return pl.pallas_call(
        exchange_kernel,
        in_specs=[anywhere, anywhere, near, near, near, near, near],
        out_specs=[anywhere, anywhere, near, near, near],
        out_shape=[jax.ShapeDtypeStruct((devices * frames, gates.shape[1]), bf16), jax.ShapeDtypeStruct((devices * frames, rest.shape[1]), bf16),
                   jax.ShapeDtypeStruct((rows, 256), bf16), jax.ShapeDtypeStruct((devices * 16, 128), bf16),
                   jax.ShapeDtypeStruct(core_out.shape, bf16)],
        scratch_shapes=gather_semaphores(devices) * 2 + [
            pltpu.VMEM((rows, 256), bf16), pltpu.VMEM((rows // 2, 256), bf16), pltpu.VMEM((n, rows // 2 // n, 256), bf16),
            dma(3), dma(3), dma(n), dma(n), dma(n), dma(n), dma(devices), dma(devices), dma(1)],
        compiler_params=pltpu.CompilerParams(collective_id=0, has_side_effects=True, vmem_limit_bytes=40 * MB),
        name="exchange",
    )(gates, rest, g_sum, in_sum, out_sum, vec, core_out)


def shifted(states):
    rows = states.shape[0]
    values = states.astype(f32)
    values = jnp.concatenate([jnp.zeros((1, values.shape[1]), f32), values[:-1]], axis=0)
    first = lax.broadcasted_iota(jnp.int32, (rows, 1), 0) % GLEN == 0
    return jnp.where(first, 0.0, values).astype(bf16)


def total_kernel(gates0, gates1, gates2, rest, sums, vec, g1c, b1c, w_in, g2c, b2c, w_up,
                 core_in, core_upper, core_loop, first_bias, upper_bias, down, down_bias, up, up_bias, in_out, out_out,
                 g1_out, b1_out, g2_out, b2_out, turned):
    hid = core_loop.shape[1]
    width = core_in.shape[0]
    rows = rest.shape[0]
    ff = up.shape[1]
    step = pl.program_id(0)
    starts = [0, width, width + hid, width + 2 * hid, width + 3 * hid]

    @pl.when(step == 0)
    def _():
        at = 0
        for l in range(3):
            turned[at:at + starts[l + 1] - starts[l], :] = rest[:, starts[l]:starts[l + 1]].T
            at += starts[l + 1] - starts[l]
            turned[at:at + hid, :] = shifted(rest[:, starts[l + 1]:starts[l + 2]]).T
            at += hid
            turned[at:at + 16, :] = jnp.ones((16, rows), bf16)
            at += 16
        begin = starts[4]
        down[...] = mm(rest[:, begin:begin + ff], rest[:, begin + ff:], 0, 0)
        short = functools.reduce(jnp.add, [vec[i:i + 16, :].astype(f32) for i in range(0, vec.shape[0], 16)])
        short = jnp.concatenate([short[i:i + 1] for i in range(16)], axis=1)
        ub = short[:, :ff]
        up_bias[...] = ub[0]
        down_bias[...] = short[0, ff:ff + width]
        mixes = short[:, ff + width:]
        grown = jnp.concatenate([sums[i * 256:(i + 1) * 256, :] for i in range(4)], axis=1).astype(f32)
        up[...] = g2c[...] * grown + b2c[...] * ub
        row = lambda a: jnp.sum(a.T, axis=0, keepdims=True)[0]
        weights = w_up[...].astype(f32)
        g2_out[...] = row(weights * grown)
        b2_out[...] = row(weights * ub)
        grown = jnp.concatenate([sums[i * 256:(i + 1) * 256, :] for i in range(4, 7)], axis=1).astype(f32)
        in_out[...] = g1c[...] * grown + b1c[...] * mixes
        weights = w_in[...].astype(f32)
        g1_out[...] = row(weights * grown)
        b1_out[...] = row(weights * mixes)
        out_out[...] = sums[7 * 256:, :].astype(f32)

    at = 0
    for l, gates in enumerate((gates0, gates1, gates2)):
        first = width if l == 0 else hid
        size = first + hid
        terms = mm(turned[at:at + size + 16, :], gates[...])
        if l == 0:
            core_in[...] = terms[:first]
            first_bias[...] = terms[size]
        else:
            core_upper[l - 1] = terms[:first]
            upper_bias[l - 1:l, :] = terms[size:size + 1]
        core_loop[l] = terms[first:size]
        at += size + 16


def run_total(gates, rest, sums, vec, g1c, b1c, w_in, g2c, b2c, w_up, hid):
    rows = gates.shape[0]
    wide_gates = 4 * hid
    ff = w_up.shape[1]
    chunk = 512
    steps = wide_gates // chunk
    one = lambda shape: (jax.ShapeDtypeStruct(shape, f32), whole(shape))
    def cut(shape):
        block = shape[:-1] + (chunk,)
        return (jax.ShapeDtypeStruct(shape, f32), pl.BlockSpec(block, lambda i: (0,) * (len(shape) - 1) + (i,)))
    outs = [cut((WIDTH, wide_gates)), cut((2, hid, wide_gates)), cut((3, hid, wide_gates)), cut((wide_gates,)), cut((2, wide_gates)),
            one((ff, WIDTH)), one((WIDTH,)), one((WIDTH, ff)), one((ff,)), one((WIDTH, 768)), one((WIDTH, WIDTH)),
            one((WIDTH,)), one((WIDTH,)), one((WIDTH,)), one((WIDTH,))]
    layer = lambda l: pl.BlockSpec((rows, chunk), lambda i: (0, l * steps + i))
    return pl.pallas_call(
        total_kernel,
        grid=(steps,),
        in_specs=[layer(0), layer(1), layer(2)] + [whole(a.shape) for a in (rest, sums, vec, g1c, b1c, w_in, g2c, b2c, w_up)],
        out_specs=[s for _, s in outs],
        out_shape=[s for s, _ in outs],
        scratch_shapes=[pltpu.VMEM((WIDTH + 5 * hid + 48, rows), bf16)],
        compiler_params=pltpu.CompilerParams(vmem_limit_bytes=60 * MB),
        name="total",
    )(gates, gates, gates, rest, sums, vec, g1c, b1c, w_in, g2c, b2c, w_up)


def on_device(entities, counts, order, first_gain, first_shift, attend_in, attend_out, second_gain, second_shift,
              up_weight, up_bias, down_weight, down_bias, core_input, core_upper, core_loop, core_first_bias,
              core_upper_bias, core_grad):
    frames = entities.shape[0]
    hid = core_loop.shape[1]
    places = jnp.broadcast_to((order % frames).astype(bf16)[:, None], (frames, 128))
    packed = jnp.concatenate([core_grad, places], axis=1)
    packed = lax.ppermute(packed, "pipe", [(0, 1), (1, 0)])
    kept = run_forward(entities, counts, first_gain[None], first_shift[None], attend_in, attend_out, second_gain[None],
                       second_shift[None], up_weight, up_bias[None])
    sums, acts, dsums = kept[10:]
    core_out, spread, scale, gates, rest, small = run_core(
        counts[:, None], sums, acts, dsums, packed, attend_out, down_weight, down_bias[None], core_input, core_upper,
        core_loop, core_first_bias[None], core_upper_bias)
    g1c, b1c, g2c, b2c = (a[:, None] for a in (first_gain, first_shift, second_gain, second_shift))
    entity_grad, g_sum, in_sum, out_sum, mix_sum = run_backward(counts, spread, scale, g1c, attend_in, attend_out, g2c, up_weight, kept[:10])
    vec = jnp.concatenate([small, mix_sum], axis=1).reshape(16, 128).astype(bf16)
    gates, rest, sums, vec, core_out = run_exchange(gates, rest, g_sum, in_sum, out_sum, vec, core_out)
    (core_in_g, core_upper_g, core_loop_g, first_bias_g, upper_bias_g, down_g, down_bias_g, up_g, up_bias_g, in_g, out_g,
     g1_g, b1_g, g2_g, b2_g) = run_total(gates, rest, sums, vec, g1c, b1c, attend_in, g2c, b2c, up_weight, hid)
    return (core_out, entity_grad, g1_g, b1_g, in_g, out_g, g2_g, b2_g, up_g, up_bias_g, down_g, down_bias_g,
            core_in_g, core_upper_g, core_loop_g, first_bias_g, upper_bias_g)


def solution(mesh):
    rows = P(("pipe", "dp"))
    return jax.shard_map(
        on_device,
        mesh=mesh,
        in_specs=(rows, rows, rows) + (P(),) * 15 + (rows,),
        out_specs=(rows, rows) + (P(),) * 15,
        check_vma=False,
    )
```

```python
import functools

import jax
import jax.numpy as jnp
from jax import lax
from jax.experimental import pallas as pl
from jax.experimental.pallas import tpu as pltpu
from jax.sharding import PartitionSpec as P

HEADS = 2
KEY = 128
SLOTS = 512
GLEN = 8
WIDTH = 256
ROWS = 8
epsilon = 1e-05
bf16 = jnp.bfloat16
f32 = jnp.float32
MB = 1 << 20
KEY_SCALE = float(KEY ** -0.5)
EXP_SCALE = float(KEY ** -0.5 * 1.4426950408889634)
CG = 0.7978845608028654


def mm(a, b, ca=1, cb=0):
    return lax.dot_general(a, b, (((ca,), (cb,)), ((), ())), preferred_element_type=f32)


def whole(shape):
    return pl.BlockSpec(shape, lambda i, *_: (0,) * len(shape))


def skewed(items, *stages):
    held = {}
    for t in range(len(items) + len(stages) - 1):
        for k in range(len(stages)):
            i = t - k
            if 0 <= i < len(items):
                held[i] = stages[k](items[i], held.get(i))
    return [held[i] for i in range(len(items))]


def gelu_pair(v):
    c = lambda x: jnp.asarray(x, bf16)
    v2 = v * v
    s = 0.5 + 0.5 * jnp.tanh(v * (CG + (CG * 0.044715) * v2))
    g = (v * s).astype(bf16)
    s = s.astype(bf16)
    d = s + (g - g * s) * (c(2 * CG) + c(6 * CG * 0.044715) * v2.astype(bf16))
    return g, d


def colsum16(n, count, a):
    rows = lax.broadcasted_iota(jnp.int32, (n, 1), 0) < count
    a = jnp.where(rows, a, jnp.asarray(0, bf16))
    t = a[:128]
    for i in range(128, n, 128):
        t = t + a[i:i + 128]
    return jnp.sum(t.astype(f32), axis=0, keepdims=True)


def wide(r):
    return jnp.concatenate([r, r], axis=1)

def stage_mix(cfg, n, ents, g1, b1, w_in, centre, ones, outs, xcs):
    RC = (cfg['RC'] if n % cfg['RC'] == 0 else n)
    items = [(f, r) for r in range(0, n, RC) for f in range(len(ents))]
    def shift(it, _):
        f, r = it
        return mm(ents[f][0, r:r + RC, :], centre[...])
    def square(it, xc):
        f, r = it
        xcs[f][r:r + RC, :] = xc
        return jnp.mean(xc * xc, axis=1, keepdims=True)
    def norm(it, var):
        f, r = it
        scale = jnp.broadcast_to(lax.rsqrt(var + epsilon), (RC, 128))
        z1 = xcs[f][r:r + RC, :] * wide(scale)
        outs[f][0][0, r:r + RC, :] = z1.astype(bf16)
        outs[f][1][0, r:r + RC, :] = scale.astype(bf16)
        return (z1 * g1[...] + b1[...]).astype(bf16)
    def mix(it, normed):
        f, r = it
        qs = mm(normed, w_in[:, :256]) * EXP_SCALE
        outs[f][2][0, r:r + RC, :256] = qs.astype(bf16)
        outs[f][2][0, r:r + RC, 256:] = mm(normed, w_in[:, 256:]).astype(bf16)
    skewed(items, shift, square, norm, mix)

def stage_attention(cfg, n, counts_, outs):
    QC = (cfg['QC'] if n % cfg['QC'] == 0 else n)
    items = [(f, h, c) for h in range(HEADS) for c in range(0, n, QC) for f in range(len(outs))]
    vts, ks = {}, {}
    for f in range(len(outs)):
        for h in range(HEADS):
            vt = outs[f][2][0, :n, (2 * HEADS + h) * KEY:(2 * HEADS + h + 1) * KEY].T
            vt = jnp.concatenate([vt, jnp.ones((16, n), bf16)], axis=0)
            vts[f, h] = jnp.where(lax.broadcasted_iota(jnp.int32, (KEY + 16, n), 1) < counts_[f], vt, jnp.asarray(0, bf16))
            k = outs[f][2][0, :n, (HEADS + h) * KEY:(HEADS + h + 1) * KEY]
            ks[f, h] = jnp.where(lax.broadcasted_iota(jnp.int32, (n, 1), 0) < counts_[f], k, k[0:1])
    def score(it, _):
        f, h, c = it
        return mm(ks[f, h], outs[f][2][0, c:c + QC, h * KEY:(h + 1) * KEY], 1, 1)
    def soft(it, s):
        f, h, c = it
        p = jnp.exp2(s - jnp.max(s, axis=0, keepdims=True)).astype(bf16)
        outs[f][3][0, h, :n, c:c + QC] = p
        return p
    def out(it, p):
        f, h, c = it
        att = mm(vts[f, h], p)
        total = att[KEY:KEY + 1]
        linv = 1.0 / total
        outs[f][5][0, h:h + 1, c:c + QC] = linv
        outs[f][4][0, h * KEY:(h + 1) * KEY, c:c + QC] = (att[:KEY] * linv).astype(bf16)
    skewed(items, score, soft, out)

def stage_mid(cfg, n, counts_, ents, w_out, w_out_c, g2, b2, ones, outs, xcs, normeds, z2ts):
    RC = (cfg['RC'] if n % cfg['RC'] == 0 else n)
    items = [(f, r) for r in range(0, n, RC) for f in range(len(ents))]
    for f in range(len(ents)):
        rowsf = jnp.where(lax.broadcasted_iota(jnp.int32, (16, n), 1) < counts_[f], 1.0, 0.0).astype(bf16)
        z2ts[f][WIDTH:, :n] = rowsf
        outs[f][10][0, 0:1] = mm(rowsf, ents[f][0, :n, :])[0:1]
        outs[f][10][0, 1:2] = mm(rowsf, outs[f][4][0, :, :n], 1, 1)[0:1]
    def proj(it, _):
        f, r = it
        att = outs[f][4][0, :, r:r + RC].T
        average = mm(att, w_out_c[...])
        return mm(att, w_out[...]) - wide(average[:, :128] + average[:, 128:]) + xcs[f][r:r + RC, :]
    def square(it, mc):
        return mc, jnp.mean(mc * mc, axis=1, keepdims=True)
    def norm(it, held):
        f, r = it
        mc, var = held
        scale = jnp.broadcast_to(lax.rsqrt(var + epsilon), (RC, 128))
        outs[f][7][0, r:r + RC, :] = scale.astype(bf16)
        z2 = mc * wide(scale)
        normeds[f][r:r + RC, :] = (z2 * g2[...] + b2[...]).astype(bf16)
        z2 = z2.astype(bf16)
        outs[f][6][0, r:r + RC, :] = z2
        rows = lax.broadcasted_iota(jnp.int32, (RC, 1), 0) + r < counts_[f]
        z2ts[f][:WIDTH, r:r + RC] = jnp.where(rows, z2, jnp.asarray(0, bf16)).T
    skewed(items, proj, square, norm)

def stage_ffn(cfg, n, counts_, normeds, z2ts, w_up, up_bias, outs):
    CH = cfg['CH']
    items = [(f, c) for c in range(0, w_up.shape[1], CH) for f in range(len(outs))]
    def up(it, _):
        f, c = it
        return mm(normeds[f][:n, :], w_up[:, c:c + CH])
    def act(it, v):
        f, c = it
        g, d = gelu_pair(v + up_bias[:, c:c + CH])
        outs[f][8][0, :n, c:c + CH] = d
        outs[f][11][0, :, c:c + CH] = colsum16(n, counts_[f], g)
        return d
    def grad(it, d):
        f, c = it
        m = mm(z2ts[f][:, :n], d)
        outs[f][9][0, :, c:c + CH] = m[:WIDTH].astype(bf16)
        outs[f][12][0, :, c:c + CH] = m[WIDTH:WIDTH + 1]
    skewed(items, up, act, grad)

FORWARD = dict(QC=512, RC=256, CH=256, F=2, parts=('mix','att','mid','ffn'))

def frame_all(cfg, n, counts_, ents, weights, outs, scratch):
    g1, b1, w_in, w_out, g2, b2, w_up, up_bias = weights
    centre, ones, w_out_c, xc, normed, z2t = scratch
    F = len(ents)
    xcs = [xc.at[f] for f in range(F)]
    normeds = [normed.at[f] for f in range(F)]
    z2ts = [z2t.at[f] for f in range(F)]
    parts = cfg['parts']
    if 'mix' in parts: stage_mix(cfg, n, ents, g1, b1, w_in, centre, ones, outs, xcs)
    if 'att' in parts:
        stage_attention(cfg, n, counts_, outs)
    if 'mid' in parts: stage_mid(cfg, n, counts_, ents, w_out, w_out_c, g2, b2, ones, outs, xcs, normeds, z2ts)
    if 'ffn' in parts: stage_ffn(cfg, n, counts_, normeds, z2ts, w_up, up_bias, outs)

def forward_kernel(cfg, counts, ent, g1, b1, w_in, w_out, g2, b2, w_up, up_bias, *rest):
    outs, scratch = rest[:13], rest[13:]
    F = cfg['F']
    step = pl.program_id(0)
    @pl.when(step == 0)
    def _():
        centre, ones, w_out_c = scratch[:3]
        same = lax.broadcasted_iota(jnp.int32, (WIDTH, WIDTH), 0) == lax.broadcasted_iota(jnp.int32, (WIDTH, WIDTH), 1)
        centre[...] = (jnp.where(same, 1.0, 0.0) - 1.0 / WIDTH).astype(bf16)
        ones[...] = jnp.full(ones.shape, 1.0 / WIDTH, bf16)
        average = jnp.broadcast_to(jnp.mean(w_out[...].astype(f32), axis=1, keepdims=True), (WIDTH, 128))
        high = average.astype(bf16)
        w_out_c[...] = jnp.concatenate([high, (average - high.astype(f32)).astype(bf16)], axis=1)
    cs = [counts[step * F + i] for i in range(F)]
    frame_all(cfg, SLOTS, cs, [ent.at[pl.ds(i, 1)] for i in range(F)], (g1, b1, w_in, w_out, g2, b2, w_up, up_bias),
              [[o.at[pl.ds(i, 1)] for o in outs] for i in range(F)], scratch)

def run_forward(entities, counts, g1, b1, w_in, w_out, g2, b2, w_up, up_bias, const=False):
    cfg = FORWARD
    frames = entities.shape[0]
    ff = w_up.shape[1]
    F = cfg['F']
    def per_frame(shape):
        return pl.BlockSpec((F,) + shape, lambda i, *_: ((0 if const else i),) + (0,) * len(shape))
    outs = [((SLOTS, WIDTH), bf16), ((SLOTS, 128), bf16), ((SLOTS, 768), bf16), ((HEADS, SLOTS, SLOTS), bf16),
            ((HEADS * KEY, SLOTS), bf16), ((HEADS, SLOTS), f32), ((SLOTS, WIDTH), bf16), ((SLOTS, 128), bf16), ((SLOTS, ff), bf16),
            ((WIDTH, ff), bf16), ((2, WIDTH), f32), ((1, ff), f32), ((1, ff), f32)]
    return pl.pallas_call(
        functools.partial(forward_kernel, cfg),
        grid_spec=pltpu.PrefetchScalarGridSpec(
            num_scalar_prefetch=1, grid=(frames // F,),
            in_specs=[per_frame((SLOTS, WIDTH))] + [whole(a.shape) for a in (g1, b1, w_in, w_out, g2, b2, w_up, up_bias)],
            out_specs=[per_frame(s) for s, _ in outs],
            scratch_shapes=[pltpu.VMEM((WIDTH, WIDTH), bf16), pltpu.VMEM((WIDTH, 128), bf16), pltpu.VMEM((WIDTH, WIDTH), bf16),
                            pltpu.VMEM((F, SLOTS, WIDTH), f32), pltpu.VMEM((F, SLOTS, WIDTH), bf16), pltpu.VMEM((F, WIDTH + 16, SLOTS), bf16)]),
        out_shape=[jax.ShapeDtypeStruct((frames,) + s, d) for s, d in outs],
        compiler_params=pltpu.CompilerParams(vmem_limit_bytes=60 * MB),
        name="encode_forward",
    )(counts, entities, g1, b1, w_in, w_out, g2, b2, w_up, up_bias)


BACKWARD = dict(QC=256, RC=256, F=2, parts=('ffn', 'att', 'mix'))

def frame_back(cfg, n, counts_, rows_, ents, weights, fr, outs, scratch):
    F = len(counts_)
    spread, scale, g_unused, w_out = weights
    entity_grad, sums_out, mix_sum = outs
    in_sum, out_sum = scratch[8:]
    upc, winc, ones, mids, ds, mixed_back, z1t, ub = scratch[:8]
    z1s, r1s, mixeds, probs, atts, linvs, z2s, r2s, dacts = fr
    parts = cfg['parts']
    RC = (cfg['RC'] if n % cfg['RC'] == 0 else n)
    QC = (cfg['QC'] if n % cfg['QC'] == 0 else n)
    dots, inners = {}, {}
    bbs = {}
    if 'ffn' in parts:
        for f in range(F):
            a = scale[rows_[f]]
            ub[f] = (upc[...] * a).astype(bf16)
        items = [(f, r) for r in range(0, n, RC) for f in range(F)]
        def up(it, _):
            f, r = it
            return mm(dacts[f][0, r:r + RC, :], ub[f], 1, 1)
        def dot(it, uc):
            f, r = it
            return uc, mm((uc * z2s[f][0, r:r + RC, :].astype(f32)).astype(bf16), ones[...])
        def mid(it, held):
            f, r = it
            uc, d = held
            r2 = r2s[f][0, r:r + RC, :].astype(f32)
            back = wide(r2) * (uc - z2s[f][0, r:r + RC, :].astype(f32) * wide(d)) + spread[rows_[f]]
            rows = lax.broadcasted_iota(jnp.int32, (RC, 1), 0) + r < counts_[f]
            back = jnp.where(rows, back, 0.0)
            mids[f, r:r + RC, :] = back
            return back.astype(bf16)
        low = dict(zip(items, skewed(items, up, dot, mid)))
        for f in range(F):
            bb = jnp.concatenate([low[f, r] for r in range(0, n, RC)], axis=0)
            bbs[f] = bb
        out_sum[...] += functools.reduce(jnp.add, [mm(atts[f][0, :, :n], bbs[f]) for f in range(F)])
    if 'att' in parts:
        for f in range(F):
            do = mm(w_out[...], bbs[f], 1, 1) if 'ffn' in parts else atts[f][0, :, :n].astype(f32)
            for h in range(HEADS):
                d = do[h * KEY:(h + 1) * KEY] * linvs[f][0, h:h + 1, :n]
                inners[f, h] = jnp.sum(d * atts[f][0, h * KEY:(h + 1) * KEY, :n].astype(f32), axis=0, keepdims=True)
                dots[f, h] = d.astype(bf16)
        items = [(f, h, c) for h in range(HEADS) for c in range(0, n, QC) for f in range(F)]
        def prob(it, _):
            f, h, c = it
            v = mixeds[f][0, :n, (2 * HEADS + h) * KEY:(2 * HEADS + h + 1) * KEY]
            return mm(v, dots[f, h][:, c:c + QC])
        def score(it, dp):
            f, h, c = it
            ds[f, h, :n, c:c + QC] = probs[f][0, h, :n, c:c + QC] * (dp - inners[f, h][:, c:c + QC]).astype(bf16)
        def finish(it, _):
            f, h, c = it
            if c + QC < n:
                return
            lo = f * n
            q = mixeds[f][0, :n, h * KEY:(h + 1) * KEY]
            rows = lax.broadcasted_iota(jnp.int32, (n, 1), 0) < counts_[f]
            k = jnp.where(rows, mixeds[f][0, :n, (HEADS + h) * KEY:(HEADS + h + 1) * KEY], jnp.asarray(0, bf16))
            d = ds[f, h, :n, :n]
            kb = jnp.where(rows, mm(d, q) * (KEY_SCALE / EXP_SCALE), 0.0)
            mixed_back[lo:lo + n, (HEADS + h) * KEY:(HEADS + h + 1) * KEY] = kb.astype(bf16)
            vb = jnp.where(rows, mm(probs[f][0, h, :n, :n], dots[f, h], 1, 1), 0.0)
            mixed_back[lo:lo + n, (2 * HEADS + h) * KEY:(2 * HEADS + h + 1) * KEY] = vb.astype(bf16)
            qt = (mm(k, d, 0, 0) * KEY_SCALE).astype(bf16)
            mixed_back[lo:lo + n, h * KEY:(h + 1) * KEY] = qt.T
        skewed(items, prob, score, finish)
    if 'mix' in parts:
        for f in range(F):
            z1t[:WIDTH, f * n:(f + 1) * n] = z1s[f][0, :n, :].T
        z1t[WIDTH:, :F * n] = jnp.ones((16, F * n), bf16)
        for c in range(0, 768, 256):
            grad = mm(z1t[:, :F * n], mixed_back[:F * n, c:c + 256])
            in_sum[:, c:c + 256] += grad[:WIDTH]
            mix_sum[:, c:c + 256] += grad[WIDTH:WIDTH + 1]
        items = [(f, r) for r in range(0, n, RC) for f in range(F)]
        def back1(it, _):
            f, r = it
            return mm(mixed_back[f * n + r:f * n + r + RC, :], winc[...], 1, 1)
        def dot1(it, uc):
            f, r = it
            return uc, mm((uc * z1s[f][0, r:r + RC, :].astype(f32)).astype(bf16), ones[...])
        def last1(it, held):
            f, r = it
            uc, d = held
            r1 = r1s[f][0, r:r + RC, :].astype(f32)
            eg = mids[f, r:r + RC, :] + wide(r1) * (uc - z1s[f][0, r:r + RC, :].astype(f32) * wide(d))
            entity_grad[f, r:r + RC, :] = eg.astype(bf16)
        skewed(items, back1, dot1, last1)
        if n < SLOTS:
            for f in range(F):
                entity_grad[f, n:, :] = jnp.zeros((SLOTS - n, WIDTH), bf16)

def backward_kernel(cfg, counts, spread, scale, g1, w_in, w_out, g2, w_up, factors, g_part, *rest):
    fr, outs, factors_all, g_all, scratch, sems, red = rest[:9], rest[9:12], rest[12], rest[13], rest[14:24], rest[24:37], rest[37:]
    F = cfg['F']
    step = pl.program_id(0)
    entity_grad, sums_out, mix_sum = outs
    in_sum, out_sum = scratch[8:]
    upc, winc, ones = scratch[:3]
    @pl.when(step == 0)
    def _():
        w = column(g2[...][None, :]) * w_up[...].astype(f32)
        upc[...] = w - jnp.mean(w, axis=0, keepdims=True)
        w = column(g1[...][None, :]) * w_in[...].astype(f32)
        winc[...] = (w - jnp.mean(w, axis=0, keepdims=True)).astype(bf16)
        ones[...] = jnp.full(ones.shape, 1.0 / WIDTH, bf16)
        for o in (in_sum, out_sum, mix_sum):
            o[...] = jnp.zeros(o.shape, f32)
    gather = make_gather(factors, factors_all, sems)
    reduce = make_reduce(red, red[10])
    todo = gather.steps()
    turns = counts.shape[0] // F
    names = [t.__name__ if hasattr(t, '__name__') else t.func.__name__ + str(t.args[0]) for t in todo]
    when = {'begin': 0, 'line_step1': 1, 'ring_step0': 1, 'line_step2': 2, 'line_step3': 3, 'far_step0': 3, 'ring_step1': 4, 'ring_step2': 5,
            'ring_step3': 6, 'far_step1': 6, 'far_step2': 7, 'far_step3': 7}
    plan = [[t for t, name in zip(todo[:-1], names) if when.get(name, turns - 1) == turn] for turn in range(turns)]
    for at, turn in enumerate(plan):
        @pl.when(step == at)
        def _(at=at, turn=turn):
            if at == 0:
                load = pltpu.make_async_copy(g_part, red[0], red[9])
                load.start()
                greet_half()
                load.wait()
            for part in turn:
                part()
            late = {0: reduce.begin, 1: reduce.spread, 3: reduce.add, 6: reduce.share, 7: reduce.finish}.get(at)
            if late is not None:
                late()
    cs = [counts[step * F + i] for i in range(F)]
    frame_back(cfg, SLOTS, cs, [pl.ds(i, 1) for i in range(F)], None, (spread.at[0], scale.at[0], None, w_out),
               [[o.at[pl.ds(i, 1)] for i in range(F)] for o in fr], outs, scratch)

    @pl.when(step == pl.num_programs(0) - 1)
    def _():
        todo[-1]()
        store = pltpu.make_async_copy(red[10], g_all, red[9])
        store.start()
        store.wait()
        for c in range(6):
            sums_out[c * 256:(c + 1) * 256, :] = in_sum[:, c * 128:(c + 1) * 128].astype(bf16)
        for c in range(2):
            sums_out[(6 + c) * 256:(7 + c) * 256, :] = out_sum[:, c * 128:(c + 1) * 128].astype(bf16)


def run_backward(counts, spread, scale, g1c, w_in, w_out, g2c, w_up, factors, g_part, kept):
    devices = 2 * lax.axis_size('dp')
    cfg = BACKWARD
    frames = kept[0].shape[0]
    ff = w_up.shape[1]
    F = cfg['F']
    def per_frame(shape):
        return pl.BlockSpec((F,) + shape, lambda i, *_: (i,) + (0,) * len(shape))
    acc = [(WIDTH, 768), (WIDTH, WIDTH)]
    return pl.pallas_call(
        functools.partial(backward_kernel, cfg),
        grid=(frames // F,),
        in_specs=[pl.BlockSpec(memory_space=pltpu.SMEM), pl.BlockSpec((1, F, WIDTH), lambda i: (i, 0, 0)), pl.BlockSpec((1, F, ff), lambda i: (i, 0, 0))]
        + [whole(a.shape) for a in (g1c, w_in, w_out, g2c, w_up)] + [pl.BlockSpec(memory_space=pl.ANY)] * 2 + [per_frame(a.shape[1:]) for a in kept],
        out_specs=[per_frame((SLOTS, WIDTH)), whole((2048, 128)), whole((1, 768)), pl.BlockSpec(memory_space=pl.ANY), pl.BlockSpec(memory_space=pl.ANY)],
        scratch_shapes=[pltpu.VMEM((WIDTH, ff), f32), pltpu.VMEM((WIDTH, 768), bf16), pltpu.VMEM((WIDTH, 128), bf16),
                            pltpu.VMEM((F, SLOTS, WIDTH), f32), pltpu.VMEM((F, HEADS, SLOTS, SLOTS), bf16), pltpu.VMEM((F * SLOTS, 768), bf16),
                            pltpu.VMEM((WIDTH + 16, F * SLOTS), bf16), pltpu.VMEM((F, WIDTH, ff), bf16)] + [pltpu.VMEM(a, f32) for a in acc] + gather_semaphores(devices) + reduce_scratch(*g_part.shape) + [pltpu.SemaphoreType.DMA, pltpu.VMEM(g_part.shape, bf16)],
        out_shape=[jax.ShapeDtypeStruct((frames, SLOTS, WIDTH), bf16), jax.ShapeDtypeStruct((2048, 128), bf16), jax.ShapeDtypeStruct((1, 768), f32),
                   jax.ShapeDtypeStruct((devices * frames, factors.shape[1]), bf16), jax.ShapeDtypeStruct(g_part.shape, bf16)],
        compiler_params=pltpu.CompilerParams(collective_id=1, has_side_effects=True, vmem_limit_bytes=60 * MB),
        name="encode_backward",
    )(counts, spread, scale, g1c, w_in, w_out, g2c, w_up, factors, g_part, *kept)


def halves(a):
    high = a.astype(bf16)
    return high, (a - high.astype(f32)).astype(bf16)

def mm_wide(a, w, cb=0):
    high, rest = halves(a)
    both = mm(jnp.concatenate([high, rest], axis=0), w, 1, cb)
    return both[:a.shape[0]] + both[a.shape[0]:]

def column(row):
    size = row.shape[-1]
    eye = lax.broadcasted_iota(jnp.int32, (size, size), 0) == lax.broadcasted_iota(jnp.int32, (size, size), 1)
    return jnp.sum(jnp.where(eye, row, 0.0), axis=1, keepdims=True)


def core_kernel(counts, m_parts, sums, acts, dsums, packed, w_out, down, down_bias, w_in, upper_far, loop_far, first_bias, upper_bias,
                core_out, spread_out, scale_out, factors, small_out, g_out, loop_t, gates_keep, cell_keep, m_near, w_upper, w_loop, load_sems):
    loads = [pltpu.make_async_copy(loop_far.at[l], w_loop.at[l], load_sems.at[l]) for l in range(3)]
    loads += [pltpu.make_async_copy(upper_far.at[l], w_upper.at[l], load_sems.at[3 + l]) for l in range(2)]
    load = pltpu.make_async_copy(m_parts, m_near, load_sems.at[5])
    for copy in (loads[0], loads[3], loads[1], loads[4], loads[2], load):
        copy.start()
    frames = sums.shape[0]
    games = frames // GLEN
    hid = w_loop.shape[1]
    depth = w_loop.shape[0]
    total = GLEN * ROWS
    wide_gates = 4 * hid
    present = column(counts[...][None, :].astype(f32))
    numer = sums[:, 0, :] + mm_wide(sums[:, 1, :], w_out[...]) + mm_wide(acts[:, 0, :], down[...])
    pooled = (numer / present + down_bias[...][None, :]).astype(bf16)
    row = lax.broadcasted_iota(jnp.int32, (total, frames), 0)
    col = lax.broadcasted_iota(jnp.int32, (total, frames), 1)
    spot = (col // GLEN == row % ROWS) & (col % GLEN == row // ROWS)
    spot = jnp.where(spot, 1.0, 0.0).astype(bf16)
    places = packed[:, hid:hid + frames].astype(f32)
    frame = lax.broadcasted_iota(jnp.int32, (frames, frames), 1).astype(f32)
    pick = jnp.where(places == frame, 1.0, 0.0).astype(bf16)
    pick = mm(spot, pick).astype(bf16)
    x = mm(pick, pooled)
    unspot = lambda a: mm(spot, a.astype(bf16), 0, 0).astype(bf16)
    ff = down.shape[0]
    width = down.shape[1]
    at = depth * wide_gates + width
    factors[:, at:at + width] = unspot(x)
    factors[:, at + width:at + width + ff] = acts[:, 0, :].astype(bf16)
    at += width + ff
    xs = [x]
    for l in range(depth):
        if l > 0:
            loads[2 + l].wait()
        w = w_in[...] if l == 0 else w_upper[l - 1]
        bias = first_bias[...][None, :] if l == 0 else upper_bias[l - 1:l, :]
        entering = (mm(x.astype(bf16), w) if l == 0 else mm_wide(x, w)) + bias
        state = jnp.zeros((ROWS, hid), f32)
        cell = jnp.zeros((ROWS, hid), f32)
        states = []
        loads[l].wait()
        for t in range(GLEN):
            gates = entering[t * ROWS:(t + 1) * ROWS]
            if t > 0:
                gates = gates + mm_wide(state, w_loop[l])
            i = 0.5 + 0.5 * jnp.tanh(0.5 * gates[:, :hid])
            f = 0.5 + 0.5 * jnp.tanh(0.5 * gates[:, hid:2 * hid])
            g = jnp.tanh(gates[:, 2 * hid:3 * hid])
            o = 0.5 + 0.5 * jnp.tanh(0.5 * gates[:, 3 * hid:])
            cell_keep[l, t, 0] = cell
            cell = f * cell + i * g
            squashed = jnp.tanh(cell)
            cell_keep[l, t, 1] = squashed
            state = o * squashed
            states.append(state)
            gates_keep[l, t] = jnp.concatenate([i, f, g, o], axis=1)
        x = jnp.concatenate(states, axis=0)
        xs.append(x)
        factors[:, at + l * hid:at + (l + 1) * hid] = unspot(x)
    core_out[...] = unspot(x)
    for l in range(depth):
        loop_t[l] = w_loop[l].T
    back = mm(spot, packed[:, :hid])
    for l in reversed(range(depth)):
        carried = jnp.zeros((ROWS, hid), f32)
        cell_carry = jnp.zeros((ROWS, hid), f32)
        gate_backs = [None] * GLEN
        for t in reversed(range(GLEN)):
            kept = gates_keep[l, t]
            i, f, g, o = [kept[:, k * hid:(k + 1) * hid] for k in range(4)]
            before, squashed = cell_keep[l, t, 0], cell_keep[l, t, 1]
            state_back = back[t * ROWS:(t + 1) * ROWS] + carried
            cell_back = state_back * (o * (1.0 - squashed * squashed)) + cell_carry
            gate_back = jnp.concatenate([cell_back * (g * i * (1.0 - i)), cell_back * (before * f * (1.0 - f)),
                                         cell_back * (i * (1.0 - g * g)), state_back * (squashed * o * (1.0 - o))], axis=1)
            cell_carry = cell_back * f
            if t > 0:
                carried = mm_wide(gate_back, loop_t[l])
            gate_backs[t] = gate_back
        gate_all = jnp.concatenate(gate_backs, axis=0)
        start = l * wide_gates
        factors[:, start:start + wide_gates] = unspot(gate_all)
        back = mm_wide(gate_all, w_in[...] if l == 0 else w_upper[l - 1], 1)
    pooled_back = mm(pick, back.astype(bf16), 0, 0)
    spread = pooled_back / present
    low = spread.astype(bf16)
    scale = mm(low, down[...], 1, 1)
    load.wait()
    for c in range(ff // 128):
        cut = slice(c * 128, (c + 1) * 128)
        g = m_near[0, :, cut].astype(f32) * scale[0:1, cut]
        for i in range(1, frames):
            g = g + m_near[i, :, cut].astype(f32) * scale[i:i + 1, cut]
        g_out[c * 256:(c + 1) * 256, :] = g.astype(bf16)
    pairs = spread_out.shape[1]
    for i in range(frames // pairs):
        spread_out[i] = spread[i * pairs:(i + 1) * pairs]
        scale_out[i] = scale[i * pairs:(i + 1) * pairs]
    factors[:, depth * wide_gates:depth * wide_gates + width] = low
    small_out[:, :ff] = jnp.sum(scale * dsums[:, 0, :], axis=0, keepdims=True)
    small_out[:, ff:] = jnp.sum(low.astype(f32) * present, axis=0, keepdims=True)


def run_core(counts, m_parts, sums, acts, dsums, packed, w_out, down, down_bias, w_in, w_upper, w_loop, first_bias, upper_bias):
    frames = sums.shape[0]
    depth, hid, wide_gates = w_loop.shape
    ff, width = down.shape
    near = pl.BlockSpec(memory_space=pltpu.VMEM)
    anywhere = pl.BlockSpec(memory_space=pl.ANY)
    pairs = BACKWARD['F']
    cols = depth * wide_gates + 2 * width + ff + depth * hid
    return pl.pallas_call(
        core_kernel,
        out_shape=[jax.ShapeDtypeStruct((frames, hid), bf16), jax.ShapeDtypeStruct((frames // pairs, pairs, width), f32),
                   jax.ShapeDtypeStruct((frames // pairs, pairs, ff), f32), jax.ShapeDtypeStruct((frames, cols), bf16),
                   jax.ShapeDtypeStruct((1, ff + width), f32), jax.ShapeDtypeStruct((WIDTH * ff // 128, 128), bf16)],
        in_specs=[near, anywhere] + [near] * 8 + [anywhere] * 2 + [near] * 2,
        scratch_shapes=[pltpu.VMEM((depth, wide_gates, hid), bf16), pltpu.VMEM((depth, GLEN, ROWS, wide_gates), f32),
                        pltpu.VMEM((depth, GLEN, 2, ROWS, hid), f32), pltpu.VMEM(m_parts.shape, bf16), pltpu.VMEM(w_upper.shape, bf16),
                        pltpu.VMEM(w_loop.shape, bf16), pltpu.SemaphoreType.DMA((6,))],
        compiler_params=pltpu.CompilerParams(vmem_limit_bytes=60 * MB),
        name="core",
    )(counts, m_parts, sums, acts, dsums, packed, w_out, down, down_bias, w_in, w_upper, w_loop, first_bias, upper_bias)


MESH = pl.DeviceIdType.MESH


def ring_place(low):
    return low ^ (low // 2)


def remote(src, dst, sems, at, pipe, dp):
    return pltpu.make_async_remote_copy(src_ref=src, dst_ref=dst, send_sem=sems[0].at[at], recv_sem=sems[1].at[at],
                                        device_id=(pipe, dp), device_id_type=MESH)


class Gather:
    def __init__(self, own, out, up, down, ahead, behind, far, over, keep):
        self.own, self.out = own, out
        self.up, self.down, self.ahead, self.behind, self.far, self.over, self.keep = up, down, ahead, behind, far, over, keep
        self.n = lax.axis_size("dp")
        self.lines = self.n // 4
        self.pipe, self.dp = lax.axis_index("pipe"), lax.axis_index("dp")
        self.z, low = self.dp // 4, self.dp % 4
        place = ring_place(low)
        spot = lambda p: ring_place(p % 4)
        self.next = spot(place + 1)
        self.prev = spot(place + 3)
        self.diag = spot(place + 2)
        self.low = low
        self.rows = own.shape[0]

    def block(self, pipe, dp):
        return self.out.at[pl.ds(pl.multiple_of((pipe * self.n + dp) * self.rows, 16), self.rows), :]

    def send(self, src, dp, sems, at, pipe, to):
        copy = remote(src, self.block(self.pipe, dp), sems, at, pipe, to)
        copy.start()
        return copy

    def spread(self, src, z, at):
        dp = z * 4 + self.low
        here = self.z * 4
        self.send(src, dp, self.ahead, at, self.pipe, here + self.next)
        self.send(src, dp, self.behind, at, self.pipe, here + self.prev)
        self.send(src, dp, self.over, at, 1 - self.pipe, self.dp)

    def begin(self):
        pltpu.make_async_copy(self.own, self.block(self.pipe, self.dp), self.keep).start()
        @pl.when(self.z + 1 < self.lines)
        def _():
            self.send(self.own, self.dp, self.up, 0, self.pipe, self.dp + 4)
        @pl.when(self.z > 0)
        def _():
            self.send(self.own, self.dp, self.down, 0, self.pipe, self.dp - 4)
        self.spread(self.own, self.z, 0)

    def wait(self, sems, at, z, low, sent):
        block = self.block(self.pipe, z * 4 + low)
        copy = remote(block, block, sems, at, self.pipe, self.dp)
        copy.wait_send() if sent else copy.wait_recv()

    def present(self, s, side):
        z = self.z - s if side == 0 else self.z + s
        return z, (z >= 0 if side == 0 else z < self.lines)

    def line_step(self, s):
        for side, sems, other in ((0, self.up, 4), (1, self.down, -4)):
            z, there = self.present(s, side)
            at = 2 * s - 1 + side
            @pl.when(there)
            def _(z=z, at=at, sems=sems, other=other, side=side):
                self.wait(sems, s - 1, z, self.low, False)
                block = self.block(self.pipe, z * 4 + self.low)
                ahead = self.z + 1 < self.lines if side == 0 else self.z > 0
                @pl.when(ahead)
                def _():
                    self.send(block, z * 4 + self.low, sems, s, self.pipe, self.dp + other)
                self.spread(block, z, at)

    def slots(self, s):
        return [(0, self.z, None)] if s == 0 else [(2 * s - 1 + side,) + self.present(s, side) for side in (0, 1)]

    def ring_step(self, s):
        for at, z, there in self.slots(s):
            def go(at=at, z=z):
                here = self.z * 4
                count = 2 * self.lines
                self.wait(self.ahead, at, z, self.prev, False)
                block = self.block(self.pipe, z * 4 + self.prev)
                if at % 2 == 0:
                    self.send(block, z * 4 + self.prev, self.far, at, self.pipe, here + self.next)
                self.send(block, z * 4 + self.prev, self.over, count + at, 1 - self.pipe, self.dp)
                self.wait(self.behind, at, z, self.next, False)
                block = self.block(self.pipe, z * 4 + self.next)
                if at % 2 == 1:
                    self.send(block, z * 4 + self.next, self.far, at, self.pipe, here + self.prev)
                self.send(block, z * 4 + self.next, self.over, 2 * count + at, 1 - self.pipe, self.dp)
            go() if there is None else pl.when(there)(go)

    def far_step(self, s):
        for at, z, there in self.slots(s):
            def go(at=at, z=z):
                self.wait(self.far, at, z, self.diag, False)
                self.send(self.block(self.pipe, z * 4 + self.diag), z * 4 + self.diag, self.over, 6 * self.lines + at, 1 - self.pipe, self.dp)
            go() if there is None else pl.when(there)(go)

    def finish(self):
        count = 2 * self.lines
        pltpu.make_async_copy(self.own, self.block(self.pipe, self.dp), self.keep).wait()
        other = 1 - self.pipe
        @pl.when(self.z + 1 < self.lines)
        def _():
            self.wait(self.up, 0, self.z, self.low, True)
        @pl.when(self.z > 0)
        def _():
            self.wait(self.down, 0, self.z, self.low, True)
        for s in range(self.lines):
            for at, z, there in self.slots(s):
                def go(at=at, z=z):
                    for group, low in enumerate((self.low, self.prev, self.next, self.diag)):
                        block = self.block(other, z * 4 + low)
                        remote(block, block, self.over, group * count + at, self.pipe, self.dp).wait()
                    self.wait(self.ahead, at, z, self.low, True)
                    self.wait(self.behind, at, z, self.low, True)
                    self.wait(self.far, at, z, self.prev if at % 2 == 0 else self.next, True)
                go() if there is None else pl.when(there)(go)
            if s > 0:
                for side, sems in ((0, self.up), (1, self.down)):
                    z, there = self.present(s, side)
                    ahead = self.z + 1 < self.lines if side == 0 else self.z > 0
                    @pl.when(there & ahead)
                    def _(z=z, sems=sems):
                        self.wait(sems, s, z, self.low, True)

    def steps(self):
        lines = self.lines
        todo = [self.begin]
        for s in range(1, lines):
            todo.append(functools.partial(self.line_step, s))
            todo.append(functools.partial(self.ring_step, s - 1))
            if s > 1:
                todo.append(functools.partial(self.far_step, s - 2))
        todo.append(functools.partial(self.ring_step, lines - 1))
        for s in range(max(lines - 2, 0), lines):
            todo.append(functools.partial(self.far_step, s))
        return todo + [self.finish]


def gather_semaphores(devices):
    lines = devices // 2 // 4
    pair = lambda n: [pltpu.SemaphoreType.DMA((n,)), pltpu.SemaphoreType.DMA((n,))]
    return pair(lines) + pair(lines) + pair(2 * lines) + pair(2 * lines) + pair(2 * lines) + pair(8 * lines) + [pltpu.SemaphoreType.DMA]


def make_gather(own, out, sems):
    p = [tuple(sems[2 * i:2 * i + 2]) for i in range(6)]
    return Gather(own, out, *p, sems[12])


def greet():
    n = lax.axis_size("dp")
    pipe, dp = lax.axis_index("pipe"), lax.axis_index("dp")
    barrier = pltpu.get_barrier_semaphore()
    for k in range(n):
        to = lax.rem(dp + k, n)
        pl.semaphore_signal(barrier, inc=1, device_id=(1 - pipe, to), device_id_type=MESH)
        if k > 0:
            pl.semaphore_signal(barrier, inc=1, device_id=(pipe, to), device_id_type=MESH)
    pl.semaphore_wait(barrier, 2 * n - 1)


def greet_half():
    n = lax.axis_size("dp")
    pipe, dp = lax.axis_index("pipe"), lax.axis_index("dp")
    barrier = pltpu.get_barrier_semaphore()
    pl.semaphore_signal(barrier, inc=1, device_id=(1 - pipe, dp), device_id_type=MESH)
    for k in range(1, n):
        pl.semaphore_signal(barrier, inc=1, device_id=(pipe, lax.rem(dp + k, n)), device_id_type=MESH)
    pl.semaphore_wait(barrier, n)


class Reduce:
    def __init__(self, big, half, parts, out, sems):
        self.big, self.half, self.parts, self.out = big, half, parts, out
        self.pair_s, self.pair_r, self.rs_s, self.rs_r, self.ag_s, self.ag_r = sems
        self.n = lax.axis_size("dp")
        self.pipe, self.dp = lax.axis_index("pipe"), lax.axis_index("dp")
        rows = big.shape[0]
        self.mid = rows // 2
        self.piece = self.mid // self.n
        self.mine = pl.ds(pl.multiple_of(self.pipe * self.mid, 16), self.mid)
        self.theirs = pl.ds(pl.multiple_of((1 - self.pipe) * self.mid, 16), self.mid)

    def pair(self, src, dst, at):
        return pltpu.make_async_remote_copy(src_ref=src, dst_ref=dst, send_sem=self.pair_s.at[at], recv_sem=self.pair_r.at[at],
                                            device_id=(1 - self.pipe, self.dp), device_id_type=MESH)

    def cut(self, owner):
        return pl.ds(pl.multiple_of(self.pipe * self.mid + owner * self.piece, 16), self.piece)

    def scatter(self, j):
        to = lax.rem(self.dp + j, self.n)
        return pltpu.make_async_remote_copy(src_ref=self.big.at[self.cut(to), :], dst_ref=self.parts.at[j], send_sem=self.rs_s.at[j],
                                            recv_sem=self.rs_r.at[j], device_id=(self.pipe, to), device_id_type=MESH)

    def collect(self, j, owner):
        to = lax.rem(self.dp + j, self.n)
        rows = self.out.at[self.cut(owner), :]
        return pltpu.make_async_remote_copy(src_ref=rows, dst_ref=rows, send_sem=self.ag_s.at[j], recv_sem=self.ag_r.at[j],
                                            device_id=(self.pipe, to), device_id_type=MESH)

    def begin(self):
        self.pair(self.big.at[self.theirs, :], self.half, 0).start()

    def spread(self):
        self.pair(self.big.at[self.theirs, :], self.half, 0).wait()
        self.big[self.mine, :] = (self.big[self.mine, :].astype(f32) + self.half[...].astype(f32)).astype(bf16)
        for j in range(1, self.n):
            self.scatter(j).start()

    def add(self):
        total = self.big[self.cut(self.dp), :].astype(f32)
        for j in range(1, self.n):
            self.scatter(j).wait_recv()
            total = total + self.parts[j].astype(f32)
        for j in range(1, self.n):
            self.scatter(j).wait_send()
        self.out[self.cut(self.dp), :] = total.astype(bf16)
        for j in range(1, self.n):
            self.collect(j, self.dp).start()

    def share(self):
        for j in range(1, self.n):
            self.collect(j, self.dp).wait_send()
            self.collect(j, lax.rem(self.dp + self.n - j, self.n)).wait_recv()
        self.pair(self.out.at[self.mine, :], self.out.at[self.mine, :], 1).start()

    def finish(self):
        self.pair(self.out.at[self.mine, :], self.out.at[self.mine, :], 1).wait_send()
        self.pair(self.out.at[self.theirs, :], self.out.at[self.theirs, :], 1).wait_recv()


def reduce_scratch(rows, cols):
    n = lax.axis_size("dp")
    dma = lambda m: pltpu.SemaphoreType.DMA((m,))
    return [pltpu.VMEM((rows, cols), bf16), pltpu.VMEM((rows // 2, cols), bf16), pltpu.VMEM((n, rows // 2 // n, cols), bf16),
            dma(2), dma(2), dma(n), dma(n), dma(n), dma(n)]


def make_reduce(scratch, out):
    return Reduce(scratch[0], scratch[1], scratch[2], out, scratch[3:9])


def exchange_kernel(sums, small, mixes, core_out, sums_all, vec_all, core_all, *scratch):
    reduce = make_reduce(scratch, sums_all)
    big = scratch[0]
    vec, swap_s, swap_r, vec_s, vec_r, keep = scratch[9:]
    n = lax.axis_size("dp")
    pipe, dp = lax.axis_index("pipe"), lax.axis_index("dp")
    load = pltpu.make_async_copy(sums, big, keep.at[1])
    load.start()
    for i in range(16):
        source, at = (small, i * 128) if (i + 1) * 128 <= small.shape[1] else (mixes, i * 128 - small.shape[1])
        vec[i:i + 1, :] = source[:, at:at + 128].astype(bf16)
    greet()
    load.wait()
    reduce.begin()
    swap = pltpu.make_async_remote_copy(src_ref=core_out, dst_ref=core_all, send_sem=swap_s.at[0], recv_sem=swap_r.at[0],
                                        device_id=(1 - pipe, dp), device_id_type=MESH)
    swap.start()
    tails = []
    own_slot = pl.ds(pl.multiple_of((pipe * n + dp) * 16, 16), 16)
    tail_keep = pltpu.make_async_copy(vec, vec_all.at[own_slot, :], keep.at[0])
    tail_keep.start()
    for j in range(1, 2 * n):
        side, step = j // n, j % n
        copy = pltpu.make_async_remote_copy(src_ref=vec, dst_ref=vec_all.at[own_slot, :], send_sem=vec_s.at[j], recv_sem=vec_r.at[j],
                                            device_id=((pipe + side) % 2, lax.rem(dp + step, n)), device_id_type=MESH)
        copy.start()
        tails.append(copy)
    reduce.spread()
    reduce.add()
    reduce.share()
    swap.wait()
    tail_keep.wait()
    for j in range(1, 2 * n):
        side, step = j // n, j % n
        tails[j - 1].wait_send()
        slot = pl.ds(pl.multiple_of((lax.rem(pipe + side, 2) * n + lax.rem(dp + n - step, n)) * 16, 16), 16)
        pltpu.make_async_remote_copy(src_ref=vec, dst_ref=vec_all.at[slot, :], send_sem=vec_s.at[j], recv_sem=vec_r.at[j],
                                     device_id=(pipe, dp), device_id_type=MESH).wait_recv()
    reduce.finish()


def run_exchange(sums, small, mixes, core_out):
    n = lax.axis_size("dp")
    devices = 2 * n
    rows, cols = sums.shape
    anywhere = pl.BlockSpec(memory_space=pl.ANY)
    near = pl.BlockSpec(memory_space=pltpu.VMEM)
    dma = lambda m: pltpu.SemaphoreType.DMA((m,))
    return pl.pallas_call(
        exchange_kernel,
        in_specs=[anywhere, near, near, near],
        out_specs=[near, near, near],
        out_shape=[jax.ShapeDtypeStruct((rows, cols), bf16), jax.ShapeDtypeStruct((devices * 16, 128), bf16),
                   jax.ShapeDtypeStruct(core_out.shape, bf16)],
        scratch_shapes=reduce_scratch(rows, cols) + [pltpu.VMEM((16, 128), bf16), dma(1), dma(1), dma(devices), dma(devices), dma(2)],
        compiler_params=pltpu.CompilerParams(collective_id=0, has_side_effects=True, vmem_limit_bytes=60 * MB),
        name="exchange",
    )(sums, small, mixes, core_out)


def shifted(states):
    rows = states.shape[0]
    values = states.astype(f32)
    values = jnp.concatenate([jnp.zeros((1, values.shape[1]), f32), values[:-1]], axis=0)
    first = lax.broadcasted_iota(jnp.int32, (rows, 1), 0) % GLEN == 0
    return jnp.where(first, 0.0, values).astype(bf16)


def total_kernel(gates0, gates1, gates2, low, start, a0, a1, a2, a3, s0, s1, s2, g_all, sums, vec, g1, b1, w_in, g2, b2, w_up,
                 core_in, core_upper, core_loop, first_bias, upper_bias, down, down_bias, up, up_bias, in_out, out_out,
                 g1_out, b1_out, g2_out, b2_out, turned):
    hid = core_loop.shape[1]
    width = core_in.shape[0]
    rows = low.shape[0]
    ff = up.shape[1]
    step = pl.program_id(0)
    @pl.when(step == 0)
    def _():
        at = 0
        entering = start[...]
        for l in range(3):
            states = (s0, s1, s2)[l][...]
            for part in (entering, shifted(states)):
                turned[at:at + part.shape[1], :] = part.T
                at += part.shape[1]
            turned[at:at + 16, :] = jnp.ones((16, rows), bf16)
            at += 16
            entering = states
        for i, part in enumerate((a0, a1, a2, a3)):
            down[i * 256:(i + 1) * 256, :] = mm(part[...], low[...], 0, 0)
        g1c, b1c, g2c, b2c = (column(a[...][None, :]) for a in (g1, b1, g2, b2))
        short = functools.reduce(jnp.add, [vec[i:i + 16, :].astype(f32) for i in range(0, vec.shape[0], 16)])
        short = jnp.concatenate([short[i:i + 1] for i in range(16)], axis=1)
        ub = short[:, :ff]
        up_bias[...] = ub[0]
        down_bias[...] = short[0, ff:ff + width]
        mixes = short[:, ff + width:]
        grown = jnp.concatenate([g_all[i * 256:(i + 1) * 256, :] for i in range(ff // 128)], axis=1).astype(f32)
        up[...] = g2c * grown + b2c * ub
        row = lambda a: jnp.sum(a.T, axis=0, keepdims=True)[0]
        weights = w_up[...].astype(f32)
        g2_out[...] = row(weights * grown)
        b2_out[...] = row(weights * ub)
        grown = jnp.concatenate([sums[i * 256:(i + 1) * 256, :] for i in range(6)], axis=1).astype(f32)
        in_out[...] = g1c * grown + b1c * mixes
        weights = w_in[...].astype(f32)
        g1_out[...] = row(weights * grown)
        b1_out[...] = row(weights * mixes)
        out_out[...] = jnp.concatenate([sums[6 * 256:7 * 256, :], sums[7 * 256:, :]], axis=1).astype(f32)

    at = 0
    for l, gates in enumerate((gates0, gates1, gates2)):
        first = width if l == 0 else hid
        size = first + hid
        terms = mm(turned[at:at + size + 16, :], gates[...])
        if l == 0:
            core_in[...] = terms[:first]
            first_bias[...] = terms[size]
        else:
            core_upper[l - 1] = terms[:first]
            upper_bias[l - 1:l, :] = terms[size:size + 1]
        core_loop[l] = terms[first:size]
        at += size + 16


def run_total(factors, g_all, sums, vec, g1, b1, w_in, g2, b2, w_up, hid):
    rows = factors.shape[0]
    wide_gates = 4 * hid
    ff = w_up.shape[1]
    chunk = 256
    steps = wide_gates // chunk
    one = lambda shape: (jax.ShapeDtypeStruct(shape, f32), whole(shape))
    def cut(shape):
        block = shape[:-1] + (chunk,)
        return (jax.ShapeDtypeStruct(shape, f32), pl.BlockSpec(block, lambda i: (0,) * (len(shape) - 1) + (i,)))
    outs = [cut((WIDTH, wide_gates)), cut((2, hid, wide_gates)), cut((3, hid, wide_gates)), cut((wide_gates,)), cut((2, wide_gates)),
            one((ff, WIDTH)), one((WIDTH,)), one((WIDTH, ff)), one((ff,)), one((WIDTH, 768)), one((WIDTH, WIDTH)),
            one((WIDTH,)), one((WIDTH,)), one((WIDTH,)), one((WIDTH,))]
    layer = lambda l: pl.BlockSpec((rows, chunk), lambda i: (0, l * steps + i))
    fixed = lambda size, at: pl.BlockSpec((rows, size), lambda i: (0, at))
    return pl.pallas_call(
        total_kernel,
        grid=(steps,),
        in_specs=[layer(0), layer(1), layer(2)] + [fixed(WIDTH, 18 + i) for i in range(6)] + [fixed(hid, 16 + i) for i in range(3)]
        + [whole(a.shape) for a in (g_all, sums, vec, g1, b1, w_in, g2, b2, w_up)],
        out_specs=[s for _, s in outs],
        out_shape=[s for s, _ in outs],
        scratch_shapes=[pltpu.VMEM((WIDTH + 5 * hid + 48, rows), bf16)],
        compiler_params=pltpu.CompilerParams(vmem_limit_bytes=60 * MB),
        name="total",
    )(*([factors] * 12), g_all, sums, vec, g1, b1, w_in, g2, b2, w_up)


def on_device(entities, counts, order, first_gain, first_shift, attend_in, attend_out, second_gain, second_shift,
              up_weight, up_bias, down_weight, down_bias, core_input, core_upper, core_loop, core_first_bias,
              core_upper_bias, core_grad):
    frames = entities.shape[0]
    hid = core_loop.shape[1]
    places = jnp.broadcast_to((order % frames).astype(bf16)[:, None], (frames, 128))
    packed = jnp.concatenate([core_grad, places], axis=1)
    packed = lax.ppermute(packed, "pipe", [(0, 1), (1, 0)])
    kept = run_forward(entities, counts, first_gain[None], first_shift[None], attend_in, attend_out, second_gain[None],
                       second_shift[None], up_weight, up_bias[None])
    sums, acts, dsums = kept[10:]
    core_out, spread, scale, factors, small, g_part = run_core(
        counts, kept[9], sums, acts, dsums, packed, attend_out, down_weight, down_bias, core_input, core_upper,
        core_loop, core_first_bias, core_upper_bias)
    entity_grad, sums, mixes, factors, g_all = run_backward(counts, spread, scale, first_gain, attend_in, attend_out, second_gain,
                                                     up_weight, factors, g_part, kept[:9])
    sums, vec, core_out = run_exchange(sums, small, mixes, core_out)
    (core_in_g, core_upper_g, core_loop_g, first_bias_g, upper_bias_g, down_g, down_bias_g, up_g, up_bias_g, in_g, out_g,
     g1_g, b1_g, g2_g, b2_g) = run_total(factors, g_all, sums, vec, first_gain, first_shift, attend_in, second_gain,
                                         second_shift, up_weight, hid)
    return (core_out, entity_grad, g1_g, b1_g, in_g, out_g, g2_g, b2_g, up_g, up_bias_g, down_g, down_bias_g,
            core_in_g, core_upper_g, core_loop_g, first_bias_g, upper_bias_g)


def solution(mesh):
    rows = P(("pipe", "dp"))
    return jax.shard_map(
        on_device,
        mesh=mesh,
        in_specs=(rows, rows, rows) + (P(),) * 15 + (rows,),
        out_specs=(rows, rows) + (P(),) * 15,
        check_vma=False,
    )
```
